512 devices in a mesh: replica: 32 (over x, z_lo, core), fsdp: 16 (over y, z_hi).
Axes of the slice: x: 4, y: 4, z: 16 (z_hi: 4, z_lo: 4; z = z_hi * 4 + z_lo), core: 2. Of those that a mesh axis runs over, the one named last changes fastest.
Arguments:
- tokens: bfloat16 [131072, 5120], P(('replica', 'fsdp')), may hold values from -6 to 6
- norm_gain: float32 [5120], replicated, may hold values from 0.25 to 1.75
- key_bias: float32 [1024], replicated, may hold values from -3 to 3
- base_weights: bfloat16 [5120, 1024], P('fsdp'), may hold values from -1 to 1, as said below
- local_weights: bfloat16 [32, 5120, 1024], P('replica', 'fsdp'), may hold values from -5 to 5
- momentum: float32 [5120, 1024], P('fsdp', 'replica'), may hold values from -0.0234375 to 0.0234375
Outputs:
- key_states: bfloat16 [131072, 1024], P(('replica', 'fsdp'))
- new_momentum: float32 [5120, 1024], P('fsdp', 'replica')
The draws below stay inside these ranges and needn't reach their ends.
Inputs may be any that keep to these rules, and one draw needn't show every extreme that they name: base_weights and local_weights are finite weights of the usual scale.
All inputs are finite; a program needn't handle non-finite values.
Results may differ from the reference program's by a relative error of at most 0.022.
Values may be sent and summed in bfloat16 or wider, within the bound.
A program may use at most 64 MiB of HBM per device.

```python
import math
import jax
import jax.numpy as jnp
from jax import lax

D = 5120
KV = 1024
REPLICAS = 32
TOKENS = 131072


def shared_base(key):
    row_scale = jnp.exp(jax.random.uniform(jax.random.fold_in(key, 101), (D, 1), jnp.float32, math.log(0.5), math.log(2.0)))
    values = jnp.clip(jax.random.normal(jax.random.fold_in(key, 102), (D, KV), jnp.float32), -4.0, 4.0)
    return values * row_scale * D ** (-0.5)


def draw_base_weights(key, part):
    return shared_base(key).astype(jnp.bfloat16)


def draw_local_weights(key, part):
    base_values = shared_base(key)
    key = jax.random.fold_in(key, 7)
    row_scale = jnp.exp(jax.random.uniform(jax.random.fold_in(key, 1), (1, D, 1), jnp.float32, math.log(0.3), math.log(3.0)))
    col_scale = jnp.exp(jax.random.uniform(jax.random.fold_in(key, 2), (1, 1, KV), jnp.float32, math.log(0.3), math.log(3.0)))
    ladder = jnp.arange(REPLICAS, dtype=jnp.float32) / max(REPLICAS - 1, 1)
    replica_scale = (0.25 * 3.0 ** ladder).reshape(REPLICAS, 1, 1)
    noise = jnp.clip(jax.random.normal(jax.random.fold_in(key, 5), (REPLICAS, D, KV), jnp.float32), -4.0, 4.0)
    drift = noise * row_scale * col_scale * replica_scale * D ** (-0.5)
    return (base_values[None] + drift).astype(jnp.bfloat16)


def block_scale(own_key, dims, shards, low, top_value):
    gain, own = 1.0, jax.random.fold_in(own_key, 6)
    for dim, parts in shards:
        steps = jnp.exp(jax.random.uniform(jax.random.fold_in(own, dim), (parts,), jnp.float32, low / len(shards), top_value / len(shards)))
        gain = gain * jnp.repeat(steps, dims[dim] // parts).reshape([-1 if axis == dim else 1 for axis in range(len(dims))])
    return gain


def normal_values(own_key, shape, deviation, bound, shards=(), kind=jnp.bfloat16):
    factor_of = block_scale(own_key, shape, shards, -0.22, 0.18) if shards else 1.0
    drawn = jax.random.normal(own_key, shape, jnp.float32) * deviation * factor_of
    return jnp.minimum(jnp.maximum(drawn, -bound), bound).astype(kind)


def setup_inputs(seed: int = 0) -> dict:
    splits = jax.random.split(jax.random.key(seed), 7)
    return {
        "tokens": normal_values(splits[0], (TOKENS, D), 1.0, 6.0, ((0, 512),)),
        "norm_gain": jnp.clip(1.0 + 0.15 * jax.random.normal(splits[1], (D,), jnp.float32), 0.25, 1.75),
        "key_bias": normal_values(splits[2], (KV,), 0.5, 3.0, (), jnp.float32),
        "base_weights": draw_base_weights(jax.random.fold_in(splits[6], 71), 0),
        "local_weights": draw_local_weights(jax.random.fold_in(splits[6], 71), 0),
        "momentum": normal_values(splits[5], (D, KV), 0.004, 0.0234375, ((0, 16), (1, 32)), jnp.float32),
    }


outer_rate = 0.7
outer_beta = 0.9
epsilon = 1e-06

def reference(tokens, norm_gain, key_bias, base_weights, local_weights, momentum):
    base_wide = base_weights.astype(jnp.float32)

    def accumulate(summed, local_one):
        quantized = lax.optimization_barrier((base_wide - local_one.astype(jnp.float32)).astype(jnp.bfloat16))
        return (summed + quantized.astype(jnp.float32), None)
    summed, _ = lax.scan(accumulate, jnp.zeros((D, KV), jnp.float32), local_weights)
    pseudo = summed / REPLICAS
    new_momentum = outer_beta * momentum + pseudo
    new_weights = (base_wide - outer_rate * (pseudo + outer_beta * new_momentum)).astype(jnp.bfloat16)

    def forward(block_tokens):
        inputs = block_tokens.astype(jnp.float32)
        normed = (inputs * lax.rsqrt(lax.optimization_barrier(jnp.mean(inputs * inputs, axis=1, keepdims=True)) + epsilon) * norm_gain).astype(jnp.bfloat16)
        product = jnp.dot(normed, new_weights, preferred_element_type=jnp.float32)
        return (product + key_bias).astype(jnp.bfloat16)
    key_states = lax.map(forward, tokens.reshape(REPLICAS, -1, D)).reshape(-1, KV)
    return (key_states, new_momentum)
```

```python
import jax
import jax.numpy as jnp
from jax import lax
from jax.experimental import pallas as pl
from jax.experimental.pallas import tpu as pltpu
from jax.sharding import PartitionSpec as P

outer_rate = 0.7
outer_beta = 0.9
epsilon = 1e-06
MESH = pl.DeviceIdType.MESH
F32, BF16 = jnp.float32, jnp.bfloat16
REPLICAS = 32
ROWS, BLK, D, KV, TOK = 320, 80, 5120, 1024, 256
HALF = KV // 2


def kernel(
    tok_hbm, gain_hbm, bias_hbm, base_hbm, local_hbm, mom_hbm,
    out_ref, nm_ref,
    tok, gain, bias, base, local, mom,
    w, nrm, acc, send_a, recv_a, send_b, recv_b, own, send_c, recv_c,
    mom_in, mom_pad, mom_t, psum, ps_send, ps_recv, o_send, o_recv,
    in_sem, ssem, rsem, mom_ssem, mom_rsem, ps_ssem, ps_rsem,
):
    r = lax.axis_index("replica")
    f = lax.axis_index("fsdp")
    x, l, c = r // 8, (r // 2) % 4, r % 2
    y, h = f // 4, f % 4
    t = 4 * c + x
    q, qi = r // 4, r % 4
    is_self = q == t

    def rep(x_, l_, c_):
        return (x_ * 4 + l_) * 2 + c_

    def to_x(k):
        return (rep((x + k) % 4, l, c), f)

    def to_y(k):
        return (r, ((y + k) % 4) * 4 + h)

    def to_h(k):
        return (r, y * 4 + (h + k) % 4)

    def to_l(k):
        return (rep(x, (l + k) % 4, c), f)

    sib = (rep(x, l, 1 - c), f)

    loads = []
    for i, (src, dst) in enumerate(
        [(base_hbm, base), (local_hbm, local), (tok_hbm, tok), (gain_hbm, gain), (bias_hbm, bias), (mom_hbm, mom)]
    ):
        cp = pltpu.make_async_copy(src, dst, in_sem.at[i])
        cp.start()
        loads.append(cp)

    bar = pltpu.get_barrier_semaphore()

    def greet(dev):
        pl.semaphore_signal(bar, inc=1, device_id=dev, device_id_type=MESH)

    greet(sib)
    for k in (1, 2, 3):
        greet(to_x(k))
        greet(to_y(k))
        greet(to_h(k))
        greet(to_l(k))

    def mom_dest(k):
        return (rep(q % 4, k, q // 4), f)

    def mom_owner(i):
        return (4 * t + i, f)

    for k in range(4):
        @pl.when(jnp.logical_not(jnp.logical_and(is_self, l == k)))
        def _():
            greet(mom_dest(k))

        @pl.when(jnp.logical_not(jnp.logical_and(is_self, qi == k)))
        def _():
            greet(mom_owner(k))

    pl.semaphore_wait(bar, 21 - 2 * is_self.astype(jnp.int32))

    count = [0]
    pending = []

    def new_id():
        count[0] += 1
        return count[0] - 1

    def remote(i, src, dst, dev):
        return pltpu.make_async_remote_copy(src, dst, ssem.at[i], rsem.at[i], device_id=dev, device_id_type=MESH)

    def send(i, src, dst, dev):
        cp = remote(i, src, dst, dev)
        cp.start()
        pending.append(cp)

    def recv(i, dst):
        remote(i, dst, dst, sib).wait_recv()

    def tile(cc, k):
        return pl.ds(pl.multiple_of(HALF * cc + 128 * ((x + k) % 4), 128), 128)

    def quant(cols):
        return (base[:, cols].astype(F32) - local[:, cols].astype(F32)).astype(BF16)

    loads[0].wait()
    loads[1].wait()
    order = (2, 1, 3, 0)
    a_id = {k: new_id() for k in order}
    for k in order:
        send_a[k] = quant(tile(1 - c, k))
        send(a_id[k], send_a.at[k], recv_a.at[k], sib)

    loads[5].wait()
    rows_of = pl.ds(pl.multiple_of(32 * qi, 32), 32)

    def mom_remote(k):
        return pltpu.make_async_remote_copy(
            mom, mom_in.at[qi], mom_ssem.at[k], mom_rsem.at[qi], device_id=mom_dest(k), device_id_type=MESH
        )

    def mom_local():
        return pltpu.make_async_copy(mom, mom_in.at[qi], mom_rsem.at[qi])

    for k in range(4):
        mine = jnp.logical_and(is_self, l == k)

        @pl.when(jnp.logical_not(mine))
        def _():
            mom_remote(k).start()

        @pl.when(mine)
        def _():
            mom_local().start()

    b_id = {k: new_id() for k in (1, 2, 3)}
    for k in order:
        part = quant(tile(c, k)).astype(F32)
        recv(a_id[k], recv_a.at[k])
        part = part + recv_a[k].astype(F32)
        if k:
            send_b[k - 1] = part.astype(BF16)
            send(b_id[k], send_b.at[k - 1], recv_b.at[k - 1], to_x(k))
        else:
            own[...] = part

    loads[2].wait()
    loads[3].wait()
    step = 16

    def norm_rows(i, carry):
        at = pl.ds(pl.multiple_of(i * step, step), step)
        v = tok[at, :].astype(F32)
        s = lax.rsqrt(jnp.mean(v * v, axis=1, keepdims=True) + epsilon)
        o = (v * s * gain[...]).astype(BF16)
        for j in range(16):
            nrm[c, j, at, :] = o[:, ROWS * j : ROWS * (j + 1)]
        return carry

    lax.fori_loop(0, TOK // step, norm_rows, 0)
    tok_id = new_id()
    send(tok_id, nrm.at[c], nrm.at[c], sib)

    for k in (1, 3, 2):
        recv(b_id[k], recv_b.at[k - 1])
    total = own[...]
    for k in (1, 2, 3):
        total = total + recv_b[k - 1].astype(F32)
    own[...] = total
    send_c[...] = total.astype(BF16)

    def rows80(l_):
        return pl.ds(pl.multiple_of(BLK * l_, 16), BLK)

    c_id = {k: new_id() for k in (1, 2, 3)}
    for k in (1, 2, 3):
        send(c_id[k], send_c.at[rows80((l + k) % 4)], recv_c.at[k - 1], to_l(k))

    for i in range(4):
        pltpu.make_async_copy(mom, mom_in.at[i], mom_rsem.at[i]).wait()
    for i in range(4):
        mom_pad[32 * i : 32 * (i + 1), 0:ROWS] = mom_in[i]
    for j in range(3):
        mom_t[128 * j : 128 * (j + 1), :] = mom_pad[:, 128 * j : 128 * (j + 1)].T
    old = mom_t[rows80(l), :]

    for k in (1, 3, 2):
        recv(c_id[k], recv_c.at[k - 1])
    pseudo = own[rows80(l), :]
    for k in (1, 2, 3):
        pseudo = pseudo + recv_c[k - 1].astype(F32)
    pseudo = pseudo / REPLICAS
    updated = outer_beta * old + pseudo
    base_own = base[rows80(l), tile(c, 0)].astype(F32)
    w[x, y, h, l] = (base_own - outer_rate * (pseudo + outer_beta * updated)).astype(BF16)

    jump = {k: new_id() for k in (1, 2, 3)}
    quad = {(g, k): new_id() for g in range(4) for k in (1, 2, 3)}

    def block(h_, l_):
        return w.at[x, y, h_, l_]

    def send_quad(g):
        b = block((h - g) % 4, l)
        for k in (2, 1, 3):
            send(quad[g, k], b, b, to_l(k))

    for k in (2, 1, 3):
        send(jump[k], block(h, l), block(h, l), to_h(k))
    send_quad(0)

    psum[0:BLK, :] = pseudo
    ps_send[...] = psum[...].T

    def ps_remote(i):
        return pltpu.make_async_remote_copy(
            ps_send.at[32 * i : 32 * (i + 1)], ps_recv.at[l], ps_ssem.at[i], ps_rsem.at[l],
            device_id=mom_owner(i), device_id_type=MESH,
        )

    def ps_local(i):
        return pltpu.make_async_copy(ps_send.at[32 * i : 32 * (i + 1)], ps_recv.at[l], ps_rsem.at[l])

    for i in range(4):
        mine = jnp.logical_and(is_self, qi == i)

        @pl.when(jnp.logical_not(mine))
        def _():
            ps_remote(i).start()

        @pl.when(mine)
        def _():
            ps_local(i).start()

    one = {(g, d, k): new_id() for g in range(4) for d in "xy" for k in (1, 2, 3)}
    two = {(g, d, k): new_id() for g in range(4) for d in "xy" for k in (1, 2, 3)}
    lo, hi, every = pl.ds(0, 2), pl.ds(2, 2), pl.ds(0, 4)

    def one_ref(g, d, k):
        hh = (h - g) % 4
        if d == "y":
            return w.at[x, (y - k) % 4, hh, lo]
        return w.at[(x - k) % 4, y, hh, hi]

    def two_ref(g, d, k):
        hh = (h - g) % 4
        if d == "x":
            return w.at[(x - k) % 4, every, hh, lo]
        return w.at[every, (y - k) % 4, hh, hi]

    def wait_quad(g):
        for k in (1, 3, 2):
            recv(quad[g, k], block((h - g) % 4, (l - k) % 4))

    def wait_jump(g):
        recv(jump[g], block((h - g) % 4, l))

    def start_one(g):
        for k in (2, 1, 3):
            for d, to in (("y", to_y), ("x", to_x)):
                ref = one_ref(g, d, 0)
                send(one[g, d, k], ref, ref, to(k))

    def start_two(g):
        for k in (1, 3, 2):
            for d in "yx":
                recv(one[g, d, k], one_ref(g, d, k))
        for k in (2, 1, 3):
            for d, to in (("x", to_x), ("y", to_y)):
                ref = two_ref(g, d, 0)
                send(two[g, d, k], ref, ref, to(k))

    def multiply(g, first):
        for k in (1, 3, 2):
            for d in "yx":
                recv(two[g, d, k], two_ref(g, d, k))
        hh = (h - g) % 4

        def part(y_, carry):
            wt = jnp.concatenate([w[i, y_, hh].reshape(ROWS, 128) for i in range(4)], axis=1)
            for cc in range(2):
                acc[cc] += jnp.dot(nrm[cc, y_ * 4 + hh], wt, preferred_element_type=F32)
            return carry

        lax.fori_loop(0, 4, part, 0)

    acc[...] = jnp.zeros_like(acc)
    wait_quad(0)
    start_one(0)
    wait_jump(1)
    send_quad(1)
    wait_jump(3)
    send_quad(3)
    wait_jump(2)
    send_quad(2)
    start_two(0)
    wait_quad(1)
    start_one(1)
    wait_quad(3)
    start_one(3)
    wait_quad(2)
    start_one(2)

    for i in range(4):
        pltpu.make_async_copy(ps_send.at[0:32], ps_recv.at[i], ps_rsem.at[i]).wait()
    for i in range(4):
        nm_ref[:, BLK * i : BLK * (i + 1)] = (
            outer_beta * mom[:, BLK * i : BLK * (i + 1)] + ps_recv[i][:, 0:BLK]
        )

    start_two(1)
    start_two(3)
    start_two(2)
    recv(tok_id, nrm.at[1 - c])
    loads[4].wait()
    for g in (0, 1, 3, 2):
        multiply(g, g == 0)

    my_cols = pl.ds(pl.multiple_of(HALF * c, 128), HALF)
    sib_cols = pl.ds(pl.multiple_of(HALF * (1 - c), 128), HALF)
    o_send[...] = (acc[1 - c] + bias[:, my_cols]).astype(BF16)
    out_id = new_id()
    send(out_id, o_send, o_recv, sib)
    out_ref[:, my_cols] = (acc[c] + bias[:, my_cols]).astype(BF16)
    recv(out_id, o_recv)
    out_ref[:, sib_cols] = o_recv[...]

    for cp in pending:
        cp.wait_send()
    for k in range(4):
        @pl.when(jnp.logical_not(jnp.logical_and(is_self, l == k)))
        def _():
            mom_remote(k).wait_send()

        @pl.when(jnp.logical_not(jnp.logical_and(is_self, qi == k)))
        def _():
            ps_remote(k).wait_send()


TRANSFERS = 4 + 3 + 1 + 3 + 3 + 12 + 24 + 24 + 1


def per_device(tokens, norm_gain, key_bias, base_weights, local_weights, momentum):
    dma = pltpu.SemaphoreType.DMA
    key_states, new_mom = pl.pallas_call(
        kernel,
        out_shape=(
            jax.ShapeDtypeStruct((TOK, KV), BF16),
            jax.ShapeDtypeStruct((32, ROWS), F32),
        ),
        in_specs=[pl.BlockSpec(memory_space=pl.ANY)] * 6,
        out_specs=(pl.BlockSpec(memory_space=pltpu.VMEM), pl.BlockSpec(memory_space=pltpu.VMEM)),
        scratch_shapes=[
            pltpu.VMEM((TOK, D), BF16),
            pltpu.VMEM((1, D), F32),
            pltpu.VMEM((1, KV), F32),
            pltpu.VMEM((ROWS, KV), BF16),
            pltpu.VMEM((ROWS, KV), BF16),
            pltpu.VMEM((32, ROWS), F32),
            pltpu.VMEM((4, 4, 4, 4, BLK, 128), BF16),
            pltpu.VMEM((2, 16, TOK, ROWS), BF16),
            pltpu.VMEM((2, TOK, HALF), F32),
            pltpu.VMEM((4, ROWS, 128), BF16),
            pltpu.VMEM((4, ROWS, 128), BF16),
            pltpu.VMEM((3, ROWS, 128), BF16),
            pltpu.VMEM((3, ROWS, 128), BF16),
            pltpu.VMEM((ROWS, 128), F32),
            pltpu.VMEM((ROWS, 128), BF16),
            pltpu.VMEM((3, BLK, 128), BF16),
            pltpu.VMEM((4, 32, ROWS), F32),
            pltpu.VMEM((128, 384), F32),
            pltpu.VMEM((384, 128), F32),
            pltpu.VMEM((128, 128), F32),
            pltpu.VMEM((128, 128), F32),
            pltpu.VMEM((4, 32, 128), F32),
            pltpu.VMEM((TOK, HALF), BF16),
            pltpu.VMEM((TOK, HALF), BF16),
            dma((6,)),
            dma((TRANSFERS,)),
            dma((TRANSFERS,)),
            dma((4,)),
            dma((4,)),
            dma((4,)),
            dma((4,)),
        ],
        compiler_params=pltpu.CompilerParams(
            collective_id=0, has_side_effects=True, vmem_limit_bytes=56 * 1024 * 1024
        ),
        name="outer_sync",
    )(
        tokens,
        norm_gain.reshape(1, D),
        key_bias.reshape(1, KV),
        base_weights,
        local_weights.reshape(ROWS, KV),
        momentum.T,
    )
    return (key_states, new_mom.T)


def solution(mesh):
    return jax.shard_map(
        per_device,
        mesh=mesh,
        in_specs=(
            P(("replica", "fsdp"), None),
            P(),
            P(),
            P("fsdp", None),
            P("replica", "fsdp", None),
            P("fsdp", "replica"),
        ),
        out_specs=(P(("replica", "fsdp"), None), P("fsdp", "replica")),
        check_vma=False,
    )
```

```python
import jax
import jax.numpy as jnp
from jax import lax
from jax.experimental import pallas as pl
from jax.experimental.pallas import tpu as pltpu
from jax.sharding import PartitionSpec as P

outer_rate = 0.7
outer_beta = 0.9
epsilon = 1e-06
MESH = pl.DeviceIdType.MESH
F32, BF16 = jnp.float32, jnp.bfloat16
REPLICAS = 32
ROWS, BLK, D, KV, TOK = 320, 80, 5120, 1024, 256
HALF = KV // 2
A = 32


def kernel(
    tok_hbm, gain_hbm, bias_hbm, base_hbm, local_hbm, mom_hbm,
    out_hbm, nm_hbm,
    tok, gain, bias, base, local, mom, nm,
    w, nrm, acc, send_a, recv_a, own_q, send_b, recv_b, own, send_c, recv_c,
    mom_send, mom_in, mom_t, psum, ps_send, ps_recv, o_send, o_own,
    in_sem, ssem, rsem, mom_ssem, mom_rsem, ps_ssem, ps_rsem,
):
    r = lax.axis_index("replica")
    f = lax.axis_index("fsdp")
    x, l, c = r // 8, (r // 2) % 4, r % 2
    y, h = f // 4, f % 4
    z = 4 * h + l
    t = 4 * c + x
    q, qi = r // 4, r % 4
    is_self = q == t

    def rep(x_, l_, c_):
        return (x_ * 4 + l_) * 2 + c_

    def to_x(k):
        return (rep((x + k) % 4, l, c), f)

    def to_y(k):
        return (r, ((y + k) % 4) * 4 + h)

    def to_h(k):
        return (r, y * 4 + (h + k) % 4)

    def to_l(k):
        return (rep(x, (l + k) % 4, c), f)

    def to_z(k):
        z_ = (z + k) % 16
        return (rep(x, z_ % 4, c), y * 4 + z_ // 4)

    sib = (rep(x, l, 1 - c), f)

    loads = []
    for i, (src, dst) in enumerate(
        [(base_hbm, base), (local_hbm, local), (mom_hbm, mom), (tok_hbm, tok), (gain_hbm, gain), (bias_hbm, bias)]
    ):
        cp = pltpu.make_async_copy(src, dst, in_sem.at[i])
        cp.start()
        loads.append(cp)

    bar = pltpu.get_barrier_semaphore()

    def greet(dev):
        pl.semaphore_signal(bar, inc=1, device_id=dev, device_id_type=MESH)

    def mom_dest(k):
        return (rep(q % 4, k, q // 4), f)

    def mom_owner(i):
        return (4 * t + i, f)

    greet(sib)
    for k in (1, 2, 3):
        greet(to_x(k))
        greet(to_y(k))
        greet(to_h(k))
        greet(to_l(k))
    greet(to_z(1))
    greet(to_z(15))
    for k in range(4):
        @pl.when(jnp.logical_not(jnp.logical_and(is_self, l == k)))
        def _():
            greet(mom_dest(k))

        @pl.when(jnp.logical_not(jnp.logical_and(is_self, qi == k)))
        def _():
            greet(mom_owner(k))

    count = [0]
    pending = []

    def new_id(n=1):
        count[0] += n
        return count[0] - n

    def remote(i, src, dst, dev):
        return pltpu.make_async_remote_copy(src, dst, ssem.at[i], rsem.at[i], device_id=dev, device_id_type=MESH)

    def send(i, src, dst, dev):
        cp = remote(i, src, dst, dev)
        cp.start()
        pending.append(cp)

    def recv(i, dst):
        remote(i, dst, dst, sib).wait_recv()

    def tile(cc, k):
        return pl.ds(pl.multiple_of(HALF * cc + 128 * ((x + k) % 4), 128), 128)

    def quant(cols):
        return (base[:, cols].astype(F32) - local[:, cols].astype(F32)).astype(BF16)

    loads[0].wait()
    loads[1].wait()
    order = (2, 1, 3, 0)
    a_id = {k: new_id() for k in order}
    for k in order:
        send_a[k] = quant(tile(1 - c, k))
    pl.semaphore_wait(bar, 23 - 2 * is_self.astype(jnp.int32))
    for k in order:
        send(a_id[k], send_a.at[k], recv_a.at[k], sib)
    for k in order:
        own_q[k] = quant(tile(c, k))

    b_id = {k: new_id() for k in (1, 2, 3)}
    for k in order:
        recv(a_id[k], recv_a.at[k])
        part = own_q[k].astype(F32) + recv_a[k].astype(F32)
        if k:
            send_b[k - 1] = part.astype(BF16)
            send(b_id[k], send_b.at[k - 1], recv_b.at[k - 1], to_x(k))
        else:
            own[...] = part

    loads[2].wait()
    for k in range(4):
        mom_send[k, :, 0:BLK] = mom[:, BLK * k : BLK * (k + 1)]

    def mom_remote(k):
        return pltpu.make_async_remote_copy(
            mom_send.at[k], mom_in.at[qi], mom_ssem.at[k], mom_rsem.at[qi], device_id=mom_dest(k), device_id_type=MESH
        )

    def mom_local(k):
        return pltpu.make_async_copy(mom_send.at[k], mom_in.at[qi], mom_rsem.at[qi])

    for k in range(4):
        mine = jnp.logical_and(is_self, l == k)

        @pl.when(jnp.logical_not(mine))
        def _():
            mom_remote(k).start()

        @pl.when(mine)
        def _():
            mom_local(k).start()

    loads[3].wait()
    loads[4].wait()
    step = 16

    def norm_rows(i, carry):
        at = pl.ds(pl.multiple_of(i * step, step), step)
        v = tok[at, :].astype(F32)
        s = lax.rsqrt(jnp.mean(v * v, axis=1, keepdims=True) + epsilon)
        o = (v * s * gain[...]).astype(BF16)
        for j in range(16):
            nrm[c, j, at, :] = o[:, ROWS * j : ROWS * (j + 1)]
        return carry

    lax.fori_loop(0, 7, norm_rows, 0)

    for k in (1, 3, 2):
        recv(b_id[k], recv_b.at[k - 1])
    total = own[...]
    for k in (1, 2, 3):
        total = total + recv_b[k - 1].astype(F32)
    own[...] = total
    send_c[...] = total.astype(BF16)

    def rows80(l_):
        return pl.ds(pl.multiple_of(BLK * l_, 16), BLK)

    c_id = {k: new_id() for k in (1, 2, 3)}
    for k in (1, 2, 3):
        send(c_id[k], send_c.at[rows80((l + k) % 4)], recv_c.at[k - 1], to_l(k))

    for i in range(4):
        pltpu.make_async_copy(mom_send.at[0], mom_in.at[i], mom_rsem.at[i]).wait()
    mom_t[...] = mom_in[...].reshape(128, 128).T
    old = mom_t[0:BLK, :]
    lax.fori_loop(7, 10, norm_rows, 0)

    for k in (1, 3, 2):
        recv(c_id[k], recv_c.at[k - 1])
    pseudo = own[rows80(l), :]
    for k in (1, 2, 3):
        pseudo = pseudo + recv_c[k - 1].astype(F32)
    pseudo = pseudo / REPLICAS
    updated = outer_beta * old + pseudo
    base_own = base[rows80(l), tile(c, 0)].astype(F32)
    w[x, y, h, l] = (base_own - outer_rate * (pseudo + outer_beta * updated)).astype(BF16)

    groups = range(4)
    ring = (2, 1, 3)
    late = (1, 3, 2)
    jump = {k: new_id() for k in ring}
    quad = {(g, k): new_id() for g in groups for k in ring}
    ax = {(g, k): new_id() for g in groups for k in ring}
    ay = {(g, k): new_id() for g in groups for k in ring}
    az = {k: new_id(4) for k in ("up", "down", "up2", "down2")}
    one = {(g, d, k): new_id() for g in groups for d in "xy" for k in ring}
    two = {(g, d, k): new_id() for g in groups for d in "xy" for k in ("up", "down", "up2", "down2")}
    a_rows, m_rows = pl.ds(0, A), pl.ds(A, BLK - A)
    lo, hi, every = pl.ds(0, 2), pl.ds(2, 2), pl.ds(0, 4)
    x_step = {"up": 1, "down": 3}

    def grp(g):
        return (h - g) % 4

    def block(g, l_):
        return w.at[x, y, grp(g), l_, m_rows]

    def send_jumps():
        b = w.at[x, y, h, l]
        for k in ring:
            send(jump[k], b, b, to_h(k))

    def wait_jump(g):
        recv(jump[g], w.at[x, y, grp(g), l])

    def send_quad(g):
        b = block(g, l)
        for k in ring:
            send(quad[g, k], b, b, to_l(k))

    def wait_quad(g):
        for k in late:
            recv(quad[g, k], block(g, (l - k) % 4))

    def send_ax(g):
        b = w.at[x, y, grp(g), l, a_rows]
        for k in ring:
            send(ax[g, k], b, b, to_x(k))

    def ax_to_ay(g):
        for k in late:
            recv(ax[g, k], w.at[(x - k) % 4, y, grp(g), l, a_rows])
        b = w.at[every, y, grp(g), l, a_rows]
        for k in ring:
            send(ay[g, k], b, b, to_y(k))

    def az_ref(h_, l_, xs=every):
        return w.at[xs, every, h_, l_, a_rows]

    def ay_to_az(g):
        for k in late:
            recv(ay[g, k], w.at[every, (y - k) % 4, grp(g), l, a_rows])
        b = az_ref(grp(g), l)
        send(az["up"] + grp(g), b, b, to_z(1))
        send(az["down"] + grp(g), b, b, to_z(15))

    def az_on(g):
        h_ = ((z + 15) % 16 // 4 - g) % 4
        recv(az["up"] + h_, az_ref(h_, (l + 3) % 4))
        b = az_ref(h_, (l + 3) % 4, lo)
        send(az["up2"] + h_, b, b, to_z(1))
        h_ = ((z + 1) % 16 // 4 - g) % 4
        recv(az["down"] + h_, az_ref(h_, (l + 1) % 4))
        b = az_ref(h_, (l + 1) % 4, hi)
        send(az["down2"] + h_, b, b, to_z(15))

    def az_end(g):
        recv(az["up2"] + grp(g), az_ref(grp(g), (l + 2) % 4, lo))
        recv(az["down2"] + grp(g), az_ref(grp(g), (l + 2) % 4, hi))

    def one_ref(g, d, k):
        if d == "y":
            return w.at[x, (y - k) % 4, grp(g), lo, m_rows]
        return w.at[(x - k) % 4, y, grp(g), hi, m_rows]

    def two_ref(g, d, k, part=every):
        if d == "x":
            return w.at[(x - k) % 4, part, grp(g), lo, m_rows]
        return w.at[part, (y - k) % 4, grp(g), hi, m_rows]

    def send_one(g):
        for k in ring:
            for d, to in (("y", to_y), ("x", to_x)):
                b = one_ref(g, d, 0)
                send(one[g, d, k], b, b, to(k))

    def one_to_two(g):
        for d, e, to in (("y", "x", to_x), ("x", "y", to_y)):
            for k in late:
                recv(one[g, d, k], one_ref(g, d, k))
            b = two_ref(g, e, 0)
            send(two[g, e, "up"], b, b, to(1))
            send(two[g, e, "down"], b, b, to(3))

    def two_on(g):
        for e, to in (("x", to_x), ("y", to_y)):
            recv(two[g, e, "up"], two_ref(g, e, 1))
            b = two_ref(g, e, 1, lo)
            send(two[g, e, "up2"], b, b, to(1))
            recv(two[g, e, "down"], two_ref(g, e, 3))
            b = two_ref(g, e, 3, hi)
            send(two[g, e, "down2"], b, b, to(3))

    def two_end(g):
        for e in "xy":
            recv(two[g, e, "up2"], two_ref(g, e, 2, lo))
            recv(two[g, e, "down2"], two_ref(g, e, 2, hi))

    def multiply(g, cc):
        def part(y_, carry):
            wt = jnp.concatenate([w[i, y_, grp(g)].reshape(ROWS, 128) for i in range(4)], axis=1)
            acc[cc] += jnp.dot(nrm[cc, y_ * 4 + grp(g)], wt, preferred_element_type=F32)
            return carry

        lax.fori_loop(0, 4, part, 0)

    send_jumps()
    send_quad(0)
    send_ax(0)

    psum[0:BLK, :] = pseudo
    ps_send[...] = psum[...].T

    def ps_remote(i):
        return pltpu.make_async_remote_copy(
            ps_send.at[32 * i : 32 * (i + 1)], ps_recv.at[l], ps_ssem.at[i], ps_rsem.at[l],
            device_id=mom_owner(i), device_id_type=MESH,
        )

    def ps_local(i):
        return pltpu.make_async_copy(ps_send.at[32 * i : 32 * (i + 1)], ps_recv.at[l], ps_rsem.at[l])

    for i in range(4):
        mine = jnp.logical_and(is_self, qi == i)

        @pl.when(jnp.logical_not(mine))
        def _():
            ps_remote(i).start()

        @pl.when(mine)
        def _():
            ps_local(i).start()

    lax.fori_loop(10, 14, norm_rows, 0)
    ax_to_ay(0)
    wait_quad(0)
    send_one(0)
    for g in (1, 3):
        wait_jump(g)
        send_quad(g)
        send_ax(g)
    lax.fori_loop(14, 16, norm_rows, 0)
    tok_id = new_id()
    send(tok_id, nrm.at[c], nrm.at[c], sib)
    ay_to_az(0)
    wait_jump(2)
    send_quad(2)
    send_ax(2)
    one_to_two(0)
    for g in (1, 3):
        ax_to_ay(g)
    for g in (1, 3):
        wait_quad(g)
        send_one(g)
    az_on(0)
    ax_to_ay(2)
    wait_quad(2)
    send_one(2)
    for g in (1, 3):
        ay_to_az(g)
    two_on(0)
    for g in (1, 3):
        one_to_two(g)
    ay_to_az(2)
    one_to_two(2)

    for i in range(4):
        pltpu.make_async_copy(ps_send.at[0:32], ps_recv.at[i], ps_rsem.at[i]).wait()
    for i in range(4):
        nm[:, BLK * i : BLK * (i + 1)] = (
            outer_beta * mom[:, BLK * i : BLK * (i + 1)] + ps_recv[i][:, 0:BLK]
        )
    nm_out = pltpu.make_async_copy(nm, nm_hbm, in_sem.at[0])
    nm_out.start()

    acc[...] = jnp.zeros_like(acc)
    recv(tok_id, nrm.at[1 - c])
    loads[5].wait()
    for g in (1, 3):
        az_on(g)
        two_on(g)
    az_on(2)
    two_end(0)
    az_end(0)
    for cc in (0, 1):
        multiply(0, cc)
    two_on(2)
    for g in (1, 3):
        two_end(g)
        az_end(g)
        for cc in (0, 1):
            multiply(g, cc)
    two_end(2)
    az_end(2)

    my_cols = pl.ds(pl.multiple_of(HALF * c, 128), HALF)
    multiply(2, 1 - c)
    o_send[...] = (acc[1 - c] + bias[:, my_cols]).astype(BF16)
    out_id = new_id()
    send(out_id, o_send, out_hbm.at[:, my_cols], sib)
    multiply(2, c)
    o_own[...] = (acc[c] + bias[:, my_cols]).astype(BF16)
    own_out = pltpu.make_async_copy(o_own, out_hbm.at[:, my_cols], in_sem.at[1])
    own_out.start()

    for cp in pending:
        cp.wait_send()
    for k in range(4):
        @pl.when(jnp.logical_not(jnp.logical_and(is_self, l == k)))
        def _():
            mom_remote(k).wait_send()

        @pl.when(jnp.logical_not(jnp.logical_and(is_self, qi == k)))
        def _():
            ps_remote(k).wait_send()
    nm_out.wait()
    own_out.wait()
    recv(out_id, out_hbm.at[:, pl.ds(pl.multiple_of(HALF * (1 - c), 128), HALF)])
    assert count[0] == TRANSFERS


TRANSFERS = 4 + 3 + 3 + 3 + 12 + 12 + 12 + 16 + 24 + 32 + 2


def per_device(tokens, norm_gain, key_bias, base_weights, local_weights, momentum):
    dma = pltpu.SemaphoreType.DMA
    key_states, new_mom = pl.pallas_call(
        kernel,
        out_shape=(
            jax.ShapeDtypeStruct((TOK, KV), BF16),
            jax.ShapeDtypeStruct((32, ROWS), F32),
        ),
        in_specs=[pl.BlockSpec(memory_space=pl.ANY)] * 6,
        out_specs=(pl.BlockSpec(memory_space=pl.ANY), pl.BlockSpec(memory_space=pl.ANY)),
        scratch_shapes=[
            pltpu.VMEM((TOK, D), BF16),
            pltpu.VMEM((1, D), F32),
            pltpu.VMEM((1, KV), F32),
            pltpu.VMEM((ROWS, KV), BF16),
            pltpu.VMEM((ROWS, KV), BF16),
            pltpu.VMEM((32, ROWS), F32),
            pltpu.VMEM((32, ROWS), F32),
            pltpu.VMEM((4, 4, 4, 4, BLK, 128), BF16),
            pltpu.VMEM((2, 16, TOK, ROWS), BF16),
            pltpu.VMEM((2, TOK, HALF), F32),
            pltpu.VMEM((4, ROWS, 128), BF16),
            pltpu.VMEM((4, ROWS, 128), BF16),
            pltpu.VMEM((4, ROWS, 128), BF16),
            pltpu.VMEM((3, ROWS, 128), BF16),
            pltpu.VMEM((3, ROWS, 128), BF16),
            pltpu.VMEM((ROWS, 128), F32),
            pltpu.VMEM((ROWS, 128), BF16),
            pltpu.VMEM((3, BLK, 128), BF16),
            pltpu.VMEM((4, 32, 128), F32),
            pltpu.VMEM((4, 32, 128), F32),
            pltpu.VMEM((128, 128), F32),
            pltpu.VMEM((128, 128), F32),
            pltpu.VMEM((128, 128), F32),
            pltpu.VMEM((4, 32, 128), F32),
            pltpu.VMEM((TOK, HALF), BF16),
            pltpu.VMEM((TOK, HALF), BF16),
            dma((6,)),
            dma((TRANSFERS,)),
            dma((TRANSFERS,)),
            dma((4,)),
            dma((4,)),
            dma((4,)),
            dma((4,)),
        ],
        compiler_params=pltpu.CompilerParams(
            collective_id=0, has_side_effects=True, vmem_limit_bytes=56 * 1024 * 1024
        ),
        name="outer_sync",
    )(
        tokens,
        norm_gain.reshape(1, D),
        key_bias.reshape(1, KV),
        base_weights,
        local_weights.reshape(ROWS, KV),
        momentum.T,
    )
    return (key_states, new_mom.T)


def solution(mesh):
    return jax.shard_map(
        per_device,
        mesh=mesh,
        in_specs=(
            P(("replica", "fsdp"), None),
            P(),
            P(),
            P("fsdp", None),
            P("replica", "fsdp", None),
            P("fsdp", "replica"),
        ),
        out_specs=(P(("replica", "fsdp"), None), P("fsdp", "replica")),
        check_vma=False,
    )
```

```python
import jax
import jax.numpy as jnp
from jax import lax
from jax.experimental import pallas as pl
from jax.experimental.pallas import tpu as pltpu
from jax.sharding import PartitionSpec as P

outer_rate = 0.7
outer_beta = 0.9
epsilon = 1e-06
MESH = pl.DeviceIdType.MESH
F32, BF16 = jnp.float32, jnp.bfloat16
REPLICAS = 32
ROWS, BLK, D, KV, TOK = 320, 80, 5120, 1024, 256
HALF = KV // 2
A = 32


def kernel(
    tok_hbm, gain_hbm, bias_hbm, base_hbm, local_hbm, mom_hbm,
    out_ref, nm_ref,
    tok, gain, bias, base, local, mom,
    w, nrm, acc, send_a, recv_a, own_q, send_b, recv_b, own, send_c, recv_c,
    mom_send, mom_in, mom_t, psum, ps_send, ps_recv, o_send,
    in_sem, ssem, rsem, mom_ssem, mom_rsem, ps_ssem, ps_rsem,
):
    r = lax.axis_index("replica")
    f = lax.axis_index("fsdp")
    x, l, c = r // 8, (r // 2) % 4, r % 2
    y, h = f // 4, f % 4
    z = 4 * h + l
    t = 4 * c + x
    q, qi = r // 4, r % 4
    is_self = q == t

    def rep(x_, l_, c_):
        return (x_ * 4 + l_) * 2 + c_

    def to_x(k):
        return (rep((x + k) % 4, l, c), f)

    def to_y(k):
        return (r, ((y + k) % 4) * 4 + h)

    def to_h(k):
        return (r, y * 4 + (h + k) % 4)

    def to_l(k):
        return (rep(x, (l + k) % 4, c), f)

    def to_z(k):
        z_ = (z + k) % 16
        return (rep(x, z_ % 4, c), y * 4 + z_ // 4)

    sib = (rep(x, l, 1 - c), f)

    loads = []
    for i, (src, dst) in enumerate(
        [(base_hbm, base), (local_hbm, local), (mom_hbm, mom), (tok_hbm, tok), (gain_hbm, gain), (bias_hbm, bias)]
    ):
        cp = pltpu.make_async_copy(src, dst, in_sem.at[i])
        cp.start()
        loads.append(cp)

    bar = pltpu.get_barrier_semaphore()

    def greet(dev):
        pl.semaphore_signal(bar, inc=1, device_id=dev, device_id_type=MESH)

    def mom_dest(k):
        return (rep(q % 4, k, q // 4), f)

    def mom_owner(i):
        return (4 * t + i, f)

    greet(sib)
    for k in (1, 2, 3):
        greet(to_x(k))
        greet(to_y(k))
        greet(to_h(k))
        greet(to_l(k))
    greet(to_z(1))
    greet(to_z(15))
    for k in range(4):
        @pl.when(jnp.logical_not(jnp.logical_and(is_self, l == k)))
        def _():
            greet(mom_dest(k))

        @pl.when(jnp.logical_not(jnp.logical_and(is_self, qi == k)))
        def _():
            greet(mom_owner(k))

    count = [0]
    pending = []

    def new_id(n=1):
        count[0] += n
        return count[0] - n

    def remote(i, src, dst, dev):
        return pltpu.make_async_remote_copy(src, dst, ssem.at[i], rsem.at[i], device_id=dev, device_id_type=MESH)

    def send(i, src, dst, dev):
        cp = remote(i, src, dst, dev)
        cp.start()
        pending.append(cp)

    def recv(i, dst):
        remote(i, dst, dst, sib).wait_recv()

    def tile(cc, k):
        return pl.ds(pl.multiple_of(HALF * cc + 128 * ((x + k) % 4), 128), 128)

    def quant(cols):
        return (base[:, cols].astype(F32) - local[:, cols].astype(F32)).astype(BF16)

    loads[0].wait()
    loads[1].wait()
    order = (2, 1, 3, 0)
    a_id = {k: new_id() for k in order}
    for k in order:
        send_a[k] = quant(tile(1 - c, k))
    pl.semaphore_wait(bar, 23 - 2 * is_self.astype(jnp.int32))
    for k in order:
        send(a_id[k], send_a.at[k], recv_a.at[k], sib)
    for k in order:
        own_q[k] = quant(tile(c, k))

    b_id = {k: new_id() for k in (1, 2, 3)}
    for k in order:
        recv(a_id[k], recv_a.at[k])
        part = own_q[k].astype(F32) + recv_a[k].astype(F32)
        if k:
            send_b[k - 1] = part.astype(BF16)
            send(b_id[k], send_b.at[k - 1], recv_b.at[k - 1], to_x(k))
        else:
            own[...] = part

    loads[2].wait()
    for k in range(4):
        mom_send[k, :, 0:BLK] = mom[:, BLK * k : BLK * (k + 1)]

    def mom_remote(k):
        return pltpu.make_async_remote_copy(
            mom_send.at[k], mom_in.at[qi], mom_ssem.at[k], mom_rsem.at[qi], device_id=mom_dest(k), device_id_type=MESH
        )

    def mom_local(k):
        return pltpu.make_async_copy(mom_send.at[k], mom_in.at[qi], mom_rsem.at[qi])

    for k in range(4):
        mine = jnp.logical_and(is_self, l == k)

        @pl.when(jnp.logical_not(mine))
        def _():
            mom_remote(k).start()

        @pl.when(mine)
        def _():
            mom_local(k).start()

    loads[3].wait()
    loads[4].wait()
    step = 16

    def norm_rows(i, carry):
        at = pl.ds(pl.multiple_of(i * step, step), step)
        v = tok[at, :].astype(F32)
        s = lax.rsqrt(jnp.mean(v * v, axis=1, keepdims=True) + epsilon)
        o = (v * s * gain[...]).astype(BF16)
        for j in range(16):
            nrm[c, j % 4, at, ROWS * (j // 4) : ROWS * (j // 4 + 1)] = o[:, ROWS * j : ROWS * (j + 1)]
        return carry

    lax.fori_loop(0, 7, norm_rows, 0)

    for k in (1, 3, 2):
        recv(b_id[k], recv_b.at[k - 1])
    total = own[...]
    for k in (1, 2, 3):
        total = total + recv_b[k - 1].astype(F32)
    own[...] = total
    send_c[...] = total.astype(BF16)

    def rows80(l_):
        return pl.ds(pl.multiple_of(BLK * l_, 16), BLK)

    c_id = {k: new_id() for k in (1, 2, 3)}
    for k in (1, 2, 3):
        send(c_id[k], send_c.at[rows80((l + k) % 4)], recv_c.at[k - 1], to_l(k))

    for i in range(4):
        pltpu.make_async_copy(mom_send.at[0], mom_in.at[i], mom_rsem.at[i]).wait()
    mom_t[...] = mom_in[...].reshape(128, 128).T
    old = mom_t[0:BLK, :]
    lax.fori_loop(7, 10, norm_rows, 0)

    for k in (1, 3, 2):
        recv(c_id[k], recv_c.at[k - 1])
    pseudo = own[rows80(l), :]
    for k in (1, 2, 3):
        pseudo = pseudo + recv_c[k - 1].astype(F32)
    pseudo = pseudo / REPLICAS
    updated = outer_beta * old + pseudo
    base_own = base[rows80(l), tile(c, 0)].astype(F32)
    w[x, h, y, l] = (base_own - outer_rate * (pseudo + outer_beta * updated)).astype(BF16)

    groups = range(4)
    ring = (2, 1, 3)
    late = (1, 3, 2)
    jump = {k: new_id() for k in ring}
    quad = {(g, k): new_id() for g in groups for k in ring}
    ax = {(g, k): new_id() for g in groups for k in ring}
    ay = {(g, k): new_id() for g in groups for k in ring}
    az = {k: new_id(4) for k in ("up", "down", "up2", "down2")}
    one = {(g, d, k): new_id() for g in groups for d in "xy" for k in ring}
    two = {(g, d, k): new_id() for g in groups for d in "xy" for k in ("up", "down", "up2", "down2")}
    a_rows, m_rows = pl.ds(0, A), pl.ds(A, BLK - A)
    lo, hi, every = pl.ds(0, 2), pl.ds(2, 2), pl.ds(0, 4)
    x_step = {"up": 1, "down": 3}

    def grp(g):
        return (h - g) % 4

    def block(g, l_):
        return w.at[x, grp(g), y, l_, m_rows]

    def send_jumps():
        b = w.at[x, h, y, l]
        for k in ring:
            send(jump[k], b, b, to_h(k))

    def wait_jump(g):
        recv(jump[g], w.at[x, grp(g), y, l])

    def send_quad(g):
        b = block(g, l)
        for k in ring:
            send(quad[g, k], b, b, to_l(k))

    def wait_quad(g):
        for k in late:
            recv(quad[g, k], block(g, (l - k) % 4))

    def send_ax(g):
        b = w.at[x, grp(g), y, l, a_rows]
        for k in ring:
            send(ax[g, k], b, b, to_x(k))

    def ax_to_ay(g):
        for k in late:
            recv(ax[g, k], w.at[(x - k) % 4, grp(g), y, l, a_rows])
        b = w.at[every, grp(g), y, l, a_rows]
        for k in ring:
            send(ay[g, k], b, b, to_y(k))

    def az_ref(h_, l_, xs=every):
        return w.at[xs, h_, every, l_, a_rows]

    def ay_to_az(g):
        for k in late:
            recv(ay[g, k], w.at[every, grp(g), (y - k) % 4, l, a_rows])
        b = az_ref(grp(g), l)
        send(az["up"] + grp(g), b, b, to_z(1))
        send(az["down"] + grp(g), b, b, to_z(15))

    def az_on(g):
        h_ = ((z + 15) % 16 // 4 - g) % 4
        recv(az["up"] + h_, az_ref(h_, (l + 3) % 4))
        b = az_ref(h_, (l + 3) % 4, lo)
        send(az["up2"] + h_, b, b, to_z(1))
        h_ = ((z + 1) % 16 // 4 - g) % 4
        recv(az["down"] + h_, az_ref(h_, (l + 1) % 4))
        b = az_ref(h_, (l + 1) % 4, hi)
        send(az["down2"] + h_, b, b, to_z(15))

    def az_end(g):
        recv(az["up2"] + grp(g), az_ref(grp(g), (l + 2) % 4, lo))
        recv(az["down2"] + grp(g), az_ref(grp(g), (l + 2) % 4, hi))

    def one_ref(g, d, k):
        if d == "y":
            return w.at[x, grp(g), (y - k) % 4, lo, m_rows]
        return w.at[(x - k) % 4, grp(g), y, hi, m_rows]

    def two_ref(g, d, k, part=every):
        if d == "x":
            return w.at[(x - k) % 4, grp(g), part, lo, m_rows]
        return w.at[part, grp(g), (y - k) % 4, hi, m_rows]

    def send_one(g):
        for k in ring:
            for d, to in (("y", to_y), ("x", to_x)):
                b = one_ref(g, d, 0)
                send(one[g, d, k], b, b, to(k))

    def one_to_two(g):
        for d, e, to in (("y", "x", to_x), ("x", "y", to_y)):
            for k in late:
                recv(one[g, d, k], one_ref(g, d, k))
            b = two_ref(g, e, 0)
            send(two[g, e, "up"], b, b, to(1))
            send(two[g, e, "down"], b, b, to(3))

    def two_on(g):
        for e, to in (("x", to_x), ("y", to_y)):
            recv(two[g, e, "up"], two_ref(g, e, 1))
            b = two_ref(g, e, 1, lo)
            send(two[g, e, "up2"], b, b, to(1))
            recv(two[g, e, "down"], two_ref(g, e, 3))
            b = two_ref(g, e, 3, hi)
            send(two[g, e, "down2"], b, b, to(3))

    def two_end(g):
        for e in "xy":
            recv(two[g, e, "up2"], two_ref(g, e, 2, lo))
            recv(two[g, e, "down2"], two_ref(g, e, 2, hi))

    def multiply(g, cc, first=False):
        for n in range(2):
            wt = jnp.concatenate([w[2 * n + i, grp(g)].reshape(4 * ROWS, 128) for i in range(2)], axis=1)
            part = jnp.dot(nrm[cc, grp(g)], wt, preferred_element_type=F32)
            cols = slice(256 * n, 256 * (n + 1))
            acc[cc, :, cols] = part if first else acc[cc, :, cols] + part

    send_jumps()
    send_quad(0)
    send_ax(0)

    psum[0:BLK, :] = pseudo
    ps_send[...] = psum[...].T

    def ps_remote(i):
        return pltpu.make_async_remote_copy(
            ps_send.at[32 * i : 32 * (i + 1)], ps_recv.at[l], ps_ssem.at[i], ps_rsem.at[l],
            device_id=mom_owner(i), device_id_type=MESH,
        )

    def ps_local(i):
        return pltpu.make_async_copy(ps_send.at[32 * i : 32 * (i + 1)], ps_recv.at[l], ps_rsem.at[l])

    for i in range(4):
        mine = jnp.logical_and(is_self, qi == i)

        @pl.when(jnp.logical_not(mine))
        def _():
            ps_remote(i).start()

        @pl.when(mine)
        def _():
            ps_local(i).start()

    lax.fori_loop(10, 14, norm_rows, 0)
    ax_to_ay(0)
    wait_quad(0)
    send_one(0)
    for g in (1, 3):
        wait_jump(g)
        send_quad(g)
        send_ax(g)
    lax.fori_loop(14, 16, norm_rows, 0)
    tok_id = new_id()
    send(tok_id, nrm.at[c], nrm.at[c], sib)
    ay_to_az(0)
    wait_jump(2)
    send_quad(2)
    send_ax(2)
    one_to_two(0)
    for g in (1, 3):
        ax_to_ay(g)
    for g in (1, 3):
        wait_quad(g)
        send_one(g)
    az_on(0)
    ax_to_ay(2)
    wait_quad(2)
    send_one(2)
    for g in (1, 3):
        ay_to_az(g)
    two_on(0)
    for g in (1, 3):
        one_to_two(g)
    ay_to_az(2)
    one_to_two(2)

    for i in range(4):
        pltpu.make_async_copy(ps_send.at[0:32], ps_recv.at[i], ps_rsem.at[i]).wait()
    for i in range(4):
        nm_ref[:, BLK * i : BLK * (i + 1)] = (
            outer_beta * mom[:, BLK * i : BLK * (i + 1)] + ps_recv[i][:, 0:BLK]
        )

    recv(tok_id, nrm.at[1 - c])
    loads[5].wait()
    for g in (1, 3):
        az_on(g)
        two_on(g)
    az_on(2)
    two_end(0)
    az_end(0)
    for cc in (0, 1):
        multiply(0, cc, True)
    two_on(2)
    for g in (1, 3):
        two_end(g)
        az_end(g)
        for cc in (0, 1):
            multiply(g, cc)
    two_end(2)
    az_end(2)

    my_cols = pl.ds(pl.multiple_of(HALF * c, 128), HALF)
    multiply(2, 1 - c)
    o_send[...] = (acc[1 - c] + bias[:, my_cols]).astype(BF16)
    out_id = new_id()
    send(out_id, o_send, out_ref.at[:, my_cols], sib)
    multiply(2, c)
    out_ref[:, my_cols] = (acc[c] + bias[:, my_cols]).astype(BF16)

    for cp in pending:
        cp.wait_send()
    for k in range(4):
        @pl.when(jnp.logical_not(jnp.logical_and(is_self, l == k)))
        def _():
            mom_remote(k).wait_send()

        @pl.when(jnp.logical_not(jnp.logical_and(is_self, qi == k)))
        def _():
            ps_remote(k).wait_send()
    recv(out_id, out_ref.at[:, pl.ds(pl.multiple_of(HALF * (1 - c), 128), HALF)])
    assert count[0] == TRANSFERS


TRANSFERS = 4 + 3 + 3 + 3 + 12 + 12 + 12 + 16 + 24 + 32 + 2


def per_device(tokens, norm_gain, key_bias, base_weights, local_weights, momentum):
    dma = pltpu.SemaphoreType.DMA
    key_states, new_mom = pl.pallas_call(
        kernel,
        out_shape=(
            pltpu.VMEM((TOK, KV), BF16),
            pltpu.VMEM((32, ROWS), F32),
        ),
        in_specs=[pl.BlockSpec(memory_space=pl.ANY)] * 6,
        out_specs=(pl.BlockSpec(memory_space=pltpu.VMEM), pl.BlockSpec(memory_space=pltpu.VMEM)),
        scratch_shapes=[
            pltpu.VMEM((TOK, D), BF16),
            pltpu.VMEM((1, D), F32),
            pltpu.VMEM((1, KV), F32),
            pltpu.VMEM((ROWS, KV), BF16),
            pltpu.VMEM((ROWS, KV), BF16),
            pltpu.VMEM((32, ROWS), F32),
            pltpu.VMEM((4, 4, 4, 4, BLK, 128), BF16),
            pltpu.VMEM((2, 4, TOK, 4 * ROWS), BF16),
            pltpu.VMEM((2, TOK, HALF), F32),
            pltpu.VMEM((4, ROWS, 128), BF16),
            pltpu.VMEM((4, ROWS, 128), BF16),
            pltpu.VMEM((4, ROWS, 128), BF16),
            pltpu.VMEM((3, ROWS, 128), BF16),
            pltpu.VMEM((3, ROWS, 128), BF16),
            pltpu.VMEM((ROWS, 128), F32),
            pltpu.VMEM((ROWS, 128), BF16),
            pltpu.VMEM((3, BLK, 128), BF16),
            pltpu.VMEM((4, 32, 128), F32),
            pltpu.VMEM((4, 32, 128), F32),
            pltpu.VMEM((128, 128), F32),
            pltpu.VMEM((128, 128), F32),
            pltpu.VMEM((128, 128), F32),
            pltpu.VMEM((4, 32, 128), F32),
            pltpu.VMEM((TOK, HALF), BF16),
            dma((6,)),
            dma((TRANSFERS,)),
            dma((TRANSFERS,)),
            dma((4,)),
            dma((4,)),
            dma((4,)),
            dma((4,)),
        ],
        compiler_params=pltpu.CompilerParams(
            collective_id=0, has_side_effects=True, vmem_limit_bytes=56 * 1024 * 1024
        ),
        name="outer_sync",
    )(
        tokens,
        norm_gain.reshape(1, D),
        key_bias.reshape(1, KV),
        base_weights,
        local_weights.reshape(ROWS, KV),
        momentum.T,
    )
    return (key_states, new_mom.T)


def solution(mesh):
    return jax.shard_map(
        per_device,
        mesh=mesh,
        in_specs=(
            P(("replica", "fsdp"), None),
            P(),
            P(),
            P("fsdp", None),
            P("replica", "fsdp", None),
            P("fsdp", "replica"),
        ),
        out_specs=(P(("replica", "fsdp"), None), P("fsdp", "replica")),
        check_vma=False,
    )
```

```python
import jax
import jax.numpy as jnp
from jax import lax
from jax.experimental import pallas as pl
from jax.experimental.pallas import tpu as pltpu
from jax.sharding import PartitionSpec as P

outer_rate = 0.7
outer_beta = 0.9
epsilon = 1e-06
MESH = pl.DeviceIdType.MESH
F32, BF16 = jnp.float32, jnp.bfloat16
REPLICAS = 32
ROWS, BLK, D, KV, TOK = 320, 80, 5120, 1024, 256
HALF = KV // 2
A = 32


def kernel(
    tok_hbm, gain_hbm, bias_hbm, base_hbm, local_hbm, mom_hbm,
    out_ref, nm_ref,
    tok, gain, bias, base, local, mom,
    w, nrm, acc, send_a, recv_a, own_q, send_b, recv_b, own, send_c, recv_c,
    mom_send, mom_in, mom_t, psum, ps_send, ps_recv, o_send,
    in_sem, ssem, rsem, mom_ssem, mom_rsem, ps_ssem, ps_rsem,
):
    r = lax.axis_index("replica")
    f = lax.axis_index("fsdp")
    x, l, c = r // 8, (r // 2) % 4, r % 2
    y, h = f // 4, f % 4
    z = 4 * h + l
    t = 4 * c + x
    q, qi = r // 4, r % 4
    is_self = q == t

    def rep(x_, l_, c_):
        return (x_ * 4 + l_) * 2 + c_

    def to_x(k):
        return (rep((x + k) % 4, l, c), f)

    def to_y(k):
        return (r, ((y + k) % 4) * 4 + h)

    def to_h(k):
        return (r, y * 4 + (h + k) % 4)

    def to_l(k):
        return (rep(x, (l + k) % 4, c), f)

    def to_z(k):
        z_ = (z + k) % 16
        return (rep(x, z_ % 4, c), y * 4 + z_ // 4)

    sib = (rep(x, l, 1 - c), f)

    loads = []
    for i, (src, dst) in enumerate(
        [(base_hbm, base), (local_hbm, local), (mom_hbm, mom), (tok_hbm, tok), (gain_hbm, gain), (bias_hbm, bias)]
    ):
        cp = pltpu.make_async_copy(src, dst, in_sem.at[i])
        cp.start()
        loads.append(cp)

    bar = pltpu.get_barrier_semaphore()

    def greet(dev):
        pl.semaphore_signal(bar, inc=1, device_id=dev, device_id_type=MESH)

    def mom_dest(k):
        return (rep(q % 4, k, q // 4), f)

    def mom_owner(i):
        return (4 * t + i, f)

    greet(to_h(1))
    greet(to_h(3))
    for k in range(4):
        @pl.when(jnp.logical_not(jnp.logical_and(is_self, l == k)))
        def _():
            greet(mom_dest(k))

        @pl.when(jnp.logical_not(jnp.logical_and(is_self, qi == k)))
        def _():
            greet(mom_owner(k))

    for k in (2, 1, 3):
        greet(to_l(k))
    for k in (2, 1, 3):
        greet(to_x(k))
        greet(to_y(k))
    greet(to_z(1))
    greet(to_z(15))
    greet(sib)

    count = [0]
    pending = []

    def new_id(n=1):
        count[0] += n
        return count[0] - n

    def remote(i, src, dst, dev):
        return pltpu.make_async_remote_copy(src, dst, ssem.at[i], rsem.at[i], device_id=dev, device_id_type=MESH)

    def send(i, src, dst, dev):
        cp = remote(i, src, dst, dev)
        cp.start()
        pending.append(cp)

    def recv(i, dst):
        remote(i, dst, dst, sib).wait_recv()

    def tile(cc, k):
        return pl.ds(pl.multiple_of(HALF * cc + 128 * ((x + k) % 4), 128), 128)

    def quant(cols):
        return (base[:, cols].astype(F32) - local[:, cols].astype(F32)).astype(BF16)

    loads[0].wait()
    loads[1].wait()
    order = (2, 1, 3, 0)
    a_id = {k: new_id() for k in order}
    for k in order:
        send_a[k] = quant(tile(1 - c, k))
    pl.semaphore_wait(bar, 22 - 2 * is_self.astype(jnp.int32))
    for k in order:
        send(a_id[k], send_a.at[k], recv_a.at[k], sib)
    for k in order:
        own_q[k] = quant(tile(c, k))

    b_id = {k: new_id() for k in (1, 2, 3)}
    for k in order:
        recv(a_id[k], recv_a.at[k])
        part = own_q[k].astype(F32) + recv_a[k].astype(F32)
        if k:
            send_b[k - 1] = part.astype(BF16)
            send(b_id[k], send_b.at[k - 1], recv_b.at[k - 1], to_x(k))
        else:
            own[...] = part

    loads[2].wait()
    for k in range(4):
        mom_send[k, :, 0:BLK] = mom[:, BLK * k : BLK * (k + 1)]

    def mom_remote(k):
        return pltpu.make_async_remote_copy(
            mom_send.at[k], mom_in.at[qi], mom_ssem.at[k], mom_rsem.at[qi], device_id=mom_dest(k), device_id_type=MESH
        )

    def mom_local(k):
        return pltpu.make_async_copy(mom_send.at[k], mom_in.at[qi], mom_rsem.at[qi])

    for k in range(4):
        mine = jnp.logical_and(is_self, l == k)

        @pl.when(jnp.logical_not(mine))
        def _():
            mom_remote(k).start()

        @pl.when(mine)
        def _():
            mom_local(k).start()

    loads[3].wait()
    loads[4].wait()
    step = 16

    def norm_rows(i, carry):
        at = pl.ds(pl.multiple_of(i * step, step), step)
        v = tok[at, :].astype(F32)
        s = lax.rsqrt(jnp.mean(v * v, axis=1, keepdims=True) + epsilon)
        o = (v * s * gain[...]).astype(BF16)
        for j in range(16):
            nrm[c, j % 4, at, ROWS * (j // 4) : ROWS * (j // 4 + 1)] = o[:, ROWS * j : ROWS * (j + 1)]
        return carry

    lax.fori_loop(0, 7, norm_rows, 0)

    for k in (1, 3, 2):
        recv(b_id[k], recv_b.at[k - 1])
    total = own[...]
    for k in (1, 2, 3):
        total = total + recv_b[k - 1].astype(F32)
    own[...] = total
    send_c[...] = total.astype(BF16)

    def rows80(l_):
        return pl.ds(pl.multiple_of(BLK * l_, 16), BLK)

    c_id = {k: new_id() for k in (1, 2, 3)}
    for k in (1, 2, 3):
        send(c_id[k], send_c.at[rows80((l + k) % 4)], recv_c.at[k - 1], to_l(k))

    for i in range(4):
        pltpu.make_async_copy(mom_send.at[0], mom_in.at[i], mom_rsem.at[i]).wait()
    mom_t[...] = mom_in[...].reshape(128, 128).T
    old = mom_t[0:BLK, :]
    lax.fori_loop(7, 10, norm_rows, 0)

    for k in (1, 3, 2):
        recv(c_id[k], recv_c.at[k - 1])
    pseudo = own[rows80(l), :]
    for k in (1, 2, 3):
        pseudo = pseudo + recv_c[k - 1].astype(F32)
    pseudo = pseudo / REPLICAS
    updated = outer_beta * old + pseudo
    base_own = base[rows80(l), tile(c, 0)].astype(F32)
    w[x, h, y, l] = (base_own - outer_rate * (pseudo + outer_beta * updated)).astype(BF16)

    groups = range(4)
    ring = (2, 1, 3)
    late = (1, 3, 2)
    jump = {k: new_id() for k in ring}
    jump2b = new_id()
    quad = {(g, k): new_id() for g in groups for k in ring}
    ax = {(g, k): new_id() for g in groups for k in ring}
    ay = {(g, k): new_id() for g in groups for k in ring}
    az = {k: new_id(4) for k in ("up", "down", "up2", "down2")}
    one = {(g, d, k): new_id() for g in groups for d in "xy" for k in ring}
    two = {(g, d, k): new_id() for g in groups for d in "xy" for k in ("up", "down", "up2", "down2")}
    a_rows, m_rows = pl.ds(0, A), pl.ds(A, BLK - A)
    lo, hi, every = pl.ds(0, 2), pl.ds(2, 2), pl.ds(0, 4)
    x_step = {"up": 1, "down": 3}

    def grp(g):
        return (h - g) % 4

    def block(g, l_):
        return w.at[x, grp(g), y, l_, m_rows]

    def send_jumps():
        b = w.at[x, h, y, l]
        for k in (1, 3):
            send(jump[k], b, b, to_h(k))

    def wait_jump(g):
        if g == 2:
            recv(jump[2], w.at[x, grp(2), y, l, pl.ds(0, 48)])
            recv(jump2b, w.at[x, grp(2), y, l, pl.ds(48, 32)])
            return
        recv(jump[g], w.at[x, grp(g), y, l])
        part = pl.ds(0, 48) if g == 1 else pl.ds(48, 32)
        b = w.at[x, grp(g), y, l, part]
        send(jump[2] if g == 1 else jump2b, b, b, to_h(g))

    def send_quad(g):
        b = block(g, l)
        for k in ring:
            send(quad[g, k], b, b, to_l(k))

    def wait_quad(g):
        for k in late:
            recv(quad[g, k], block(g, (l - k) % 4))

    def send_ax(g):
        b = w.at[x, grp(g), y, l, a_rows]
        for k in ring:
            send(ax[g, k], b, b, to_x(k))

    def ax_to_ay(g):
        for k in late:
            recv(ax[g, k], w.at[(x - k) % 4, grp(g), y, l, a_rows])
        b = w.at[every, grp(g), y, l, a_rows]
        for k in ring:
            send(ay[g, k], b, b, to_y(k))

    def az_ref(h_, l_, xs=every):
        return w.at[xs, h_, every, l_, a_rows]

    def ay_to_az(g):
        for k in late:
            recv(ay[g, k], w.at[every, grp(g), (y - k) % 4, l, a_rows])
        b = az_ref(grp(g), l)
        send(az["up"] + grp(g), b, b, to_z(1))
        send(az["down"] + grp(g), b, b, to_z(15))

    def az_on(g):
        h_ = ((z + 15) % 16 // 4 - g) % 4
        recv(az["up"] + h_, az_ref(h_, (l + 3) % 4))
        b = az_ref(h_, (l + 3) % 4, lo)
        send(az["up2"] + h_, b, b, to_z(1))
        h_ = ((z + 1) % 16 // 4 - g) % 4
        recv(az["down"] + h_, az_ref(h_, (l + 1) % 4))
        b = az_ref(h_, (l + 1) % 4, hi)
        send(az["down2"] + h_, b, b, to_z(15))

    def az_end(g):
        recv(az["up2"] + grp(g), az_ref(grp(g), (l + 2) % 4, lo))
        recv(az["down2"] + grp(g), az_ref(grp(g), (l + 2) % 4, hi))

    def one_ref(g, d, k):
        if d == "y":
            return w.at[x, grp(g), (y - k) % 4, lo, m_rows]
        return w.at[(x - k) % 4, grp(g), y, hi, m_rows]

    def two_ref(g, d, k, part=every):
        if d == "x":
            return w.at[(x - k) % 4, grp(g), part, lo, m_rows]
        return w.at[part, grp(g), (y - k) % 4, hi, m_rows]

    def send_one(g):
        for k in ring:
            for d, to in (("y", to_y), ("x", to_x)):
                b = one_ref(g, d, 0)
                send(one[g, d, k], b, b, to(k))

    def one_to_two(g):
        for d, e, to in (("y", "x", to_x), ("x", "y", to_y)):
            for k in late:
                recv(one[g, d, k], one_ref(g, d, k))
            b = two_ref(g, e, 0)
            send(two[g, e, "up"], b, b, to(1))
            send(two[g, e, "down"], b, b, to(3))

    def two_on(g):
        for e, to in (("x", to_x), ("y", to_y)):
            recv(two[g, e, "up"], two_ref(g, e, 1))
            b = two_ref(g, e, 1, lo)
            send(two[g, e, "up2"], b, b, to(1))
            recv(two[g, e, "down"], two_ref(g, e, 3))
            b = two_ref(g, e, 3, hi)
            send(two[g, e, "down2"], b, b, to(3))

    def two_end(g):
        for e in "xy":
            recv(two[g, e, "up2"], two_ref(g, e, 2, lo))
            recv(two[g, e, "down2"], two_ref(g, e, 2, hi))

    def multiply(g, cc, first=False):
        for n in range(2):
            wt = jnp.concatenate([w[2 * n + i, grp(g)].reshape(4 * ROWS, 128) for i in range(2)], axis=1)
            part = jnp.dot(nrm[cc, grp(g)], wt, preferred_element_type=F32)
            cols = slice(256 * n, 256 * (n + 1))
            acc[cc, :, cols] = part if first else acc[cc, :, cols] + part

    send_quad(0)
    send_jumps()
    send_ax(0)

    lax.fori_loop(10, 14, norm_rows, 0)
    ax_to_ay(0)
    wait_quad(0)
    send_one(0)
    for g in (1, 3):
        wait_jump(g)
        send_quad(g)
        send_ax(g)
    lax.fori_loop(14, 16, norm_rows, 0)
    tok_id = new_id()
    send(tok_id, nrm.at[c], nrm.at[c], sib)
    ay_to_az(0)
    wait_jump(2)
    send_quad(2)
    send_ax(2)
    one_to_two(0)
    for g in (1, 3):
        ax_to_ay(g)
    for g in (1, 3):
        wait_quad(g)
        send_one(g)
    az_on(0)
    ax_to_ay(2)
    wait_quad(2)
    send_one(2)
    for g in (1, 3):
        ay_to_az(g)
    two_on(0)
    for g in (1, 3):
        one_to_two(g)
    ay_to_az(2)
    one_to_two(2)

    psum[0:BLK, :] = pseudo
    ps_send[...] = psum[...].T

    def ps_remote(i):
        return pltpu.make_async_remote_copy(
            ps_send.at[32 * i : 32 * (i + 1)], ps_recv.at[l], ps_ssem.at[i], ps_rsem.at[l],
            device_id=mom_owner(i), device_id_type=MESH,
        )

    def ps_local(i):
        return pltpu.make_async_copy(ps_send.at[32 * i : 32 * (i + 1)], ps_recv.at[l], ps_rsem.at[l])

    for i in range(4):
        mine = jnp.logical_and(is_self, qi == i)

        @pl.when(jnp.logical_not(mine))
        def _():
            ps_remote(i).start()

        @pl.when(mine)
        def _():
            ps_local(i).start()

    recv(tok_id, nrm.at[1 - c])
    loads[5].wait()
    for g in (1, 3):
        az_on(g)
        two_on(g)
    az_on(2)
    two_end(0)
    az_end(0)
    for cc in (0, 1):
        multiply(0, cc, True)
    two_on(2)
    for g in (1, 3):
        two_end(g)
        az_end(g)
        for cc in (0, 1):
            multiply(g, cc)
    for i in range(4):
        pltpu.make_async_copy(ps_send.at[0:32], ps_recv.at[i], ps_rsem.at[i]).wait()
    for i in range(4):
        nm_ref[:, BLK * i : BLK * (i + 1)] = (
            outer_beta * mom[:, BLK * i : BLK * (i + 1)] + ps_recv[i][:, 0:BLK]
        )

    two_end(2)
    az_end(2)

    my_cols = pl.ds(pl.multiple_of(HALF * c, 128), HALF)
    multiply(2, 1 - c)
    o_send[...] = (acc[1 - c] + bias[:, my_cols]).astype(BF16)
    out_id = new_id()
    send(out_id, o_send, out_ref.at[:, my_cols], sib)
    multiply(2, c)
    out_ref[:, my_cols] = (acc[c] + bias[:, my_cols]).astype(BF16)

    for cp in pending:
        cp.wait_send()
    for k in range(4):
        @pl.when(jnp.logical_not(jnp.logical_and(is_self, l == k)))
        def _():
            mom_remote(k).wait_send()

        @pl.when(jnp.logical_not(jnp.logical_and(is_self, qi == k)))
        def _():
            ps_remote(k).wait_send()
    recv(out_id, out_ref.at[:, pl.ds(pl.multiple_of(HALF * (1 - c), 128), HALF)])
    assert count[0] == TRANSFERS


TRANSFERS = 5 + 3 + 3 + 3 + 12 + 12 + 12 + 16 + 24 + 32 + 2


def per_device(tokens, norm_gain, key_bias, base_weights, local_weights, momentum):
    dma = pltpu.SemaphoreType.DMA
    key_states, new_mom = pl.pallas_call(
        kernel,
        out_shape=(
            pltpu.VMEM((TOK, KV), BF16),
            pltpu.VMEM((32, ROWS), F32),
        ),
        in_specs=[pl.BlockSpec(memory_space=pl.ANY)] * 6,
        out_specs=(pl.BlockSpec(memory_space=pltpu.VMEM), pl.BlockSpec(memory_space=pltpu.VMEM)),
        scratch_shapes=[
            pltpu.VMEM((TOK, D), BF16),
            pltpu.VMEM((1, D), F32),
            pltpu.VMEM((1, KV), F32),
            pltpu.VMEM((ROWS, KV), BF16),
            pltpu.VMEM((ROWS, KV), BF16),
            pltpu.VMEM((32, ROWS), F32),
            pltpu.VMEM((4, 4, 4, 4, BLK, 128), BF16),
            pltpu.VMEM((2, 4, TOK, 4 * ROWS), BF16),
            pltpu.VMEM((2, TOK, HALF), F32),
            pltpu.VMEM((4, ROWS, 128), BF16),
            pltpu.VMEM((4, ROWS, 128), BF16),
            pltpu.VMEM((4, ROWS, 128), BF16),
            pltpu.VMEM((3, ROWS, 128), BF16),
            pltpu.VMEM((3, ROWS, 128), BF16),
            pltpu.VMEM((ROWS, 128), F32),
            pltpu.VMEM((ROWS, 128), BF16),
            pltpu.VMEM((3, BLK, 128), BF16),
            pltpu.VMEM((4, 32, 128), F32),
            pltpu.VMEM((4, 32, 128), F32),
            pltpu.VMEM((128, 128), F32),
            pltpu.VMEM((128, 128), F32),
            pltpu.VMEM((128, 128), F32),
            pltpu.VMEM((4, 32, 128), F32),
            pltpu.VMEM((TOK, HALF), BF16),
            dma((6,)),
            dma((TRANSFERS,)),
            dma((TRANSFERS,)),
            dma((4,)),
            dma((4,)),
            dma((4,)),
            dma((4,)),
        ],
        compiler_params=pltpu.CompilerParams(
            collective_id=0, has_side_effects=True, vmem_limit_bytes=56 * 1024 * 1024
        ),
        name="outer_sync",
    )(
        tokens,
        norm_gain.reshape(1, D),
        key_bias.reshape(1, KV),
        base_weights,
        local_weights.reshape(ROWS, KV),
        momentum.T,
    )
    return (key_states, new_mom.T)


def solution(mesh):
    return jax.shard_map(
        per_device,
        mesh=mesh,
        in_specs=(
            P(("replica", "fsdp"), None),
            P(),
            P(),
            P("fsdp", None),
            P("replica", "fsdp", None),
            P("fsdp", "replica"),
        ),
        out_specs=(P(("replica", "fsdp"), None), P("fsdp", "replica")),
        check_vma=False,
    )
```

```python
import jax
import jax.numpy as jnp
from jax import lax
from jax.experimental import pallas as pl
from jax.experimental.pallas import tpu as pltpu
from jax.sharding import PartitionSpec as P

outer_rate = 0.7
outer_beta = 0.9
epsilon = 1e-06
MESH = pl.DeviceIdType.MESH
F32, BF16 = jnp.float32, jnp.bfloat16
REPLICAS = 32
ROWS, BLK, D, KV, TOK = 320, 80, 5120, 1024, 256
HALF = KV // 2
A = 32


def kernel(
    tok_hbm, gain_hbm, bias_hbm, base_hbm, local_hbm, mom_hbm,
    out_ref, nm_ref,
    tok, gain, bias, base, local, mom,
    w, nrm, acc, send_a, recv_a, own_q, send_b, recv_b, own, send_c, recv_c,
    mom_send, mom_in, mom_t, psum, ps_send, ps_recv, o_send,
    in_sem, ssem, rsem, mom_ssem, mom_rsem, ps_ssem, ps_rsem,
):
    r = lax.axis_index("replica")
    f = lax.axis_index("fsdp")
    x, l, c = r // 8, (r // 2) % 4, r % 2
    y, h = f // 4, f % 4
    z = 4 * h + l
    t = 4 * c + x
    q, qi = r // 4, r % 4
    is_self = q == t

    def rep(x_, l_, c_):
        return (x_ * 4 + l_) * 2 + c_

    def to_x(k):
        return (rep((x + k) % 4, l, c), f)

    def to_y(k):
        return (r, ((y + k) % 4) * 4 + h)

    def to_h(k):
        return (r, y * 4 + (h + k) % 4)

    def to_l(k):
        return (rep(x, (l + k) % 4, c), f)

    def to_z(k):
        z_ = (z + k) % 16
        return (rep(x, z_ % 4, c), y * 4 + z_ // 4)

    sib = (rep(x, l, 1 - c), f)

    loads = []
    for i, (src, dst) in enumerate(
        [(base_hbm, base), (local_hbm, local), (mom_hbm, mom), (tok_hbm, tok), (gain_hbm, gain), (bias_hbm, bias)]
    ):
        cp = pltpu.make_async_copy(src, dst, in_sem.at[i])
        cp.start()
        loads.append(cp)

    bar = pltpu.get_barrier_semaphore()

    def greet(dev):
        pl.semaphore_signal(bar, inc=1, device_id=dev, device_id_type=MESH)

    def mom_dest(k):
        return (rep(q % 4, k, q // 4), f)

    def mom_owner(i):
        return (4 * t + i, f)

    greet(to_h(1))
    greet(to_h(3))
    for k in range(4):
        @pl.when(jnp.logical_not(jnp.logical_and(is_self, l == k)))
        def _():
            greet(mom_dest(k))

        @pl.when(jnp.logical_not(jnp.logical_and(is_self, qi == k)))
        def _():
            greet(mom_owner(k))

    for k in (2, 1, 3):
        greet(to_l(k))
    for k in (2, 1, 3):
        greet(to_x(k))
        greet(to_y(k))
    greet(to_z(1))
    greet(to_z(15))
    greet(to_z(2))
    greet(to_z(14))
    greet(sib)

    count = [0]
    pending = []

    def new_id(n=1):
        count[0] += n
        return count[0] - n

    def remote(i, src, dst, dev):
        return pltpu.make_async_remote_copy(src, dst, ssem.at[i], rsem.at[i], device_id=dev, device_id_type=MESH)

    def send(i, src, dst, dev):
        cp = remote(i, src, dst, dev)
        cp.start()
        pending.append(cp)

    def recv(i, dst):
        remote(i, dst, dst, sib).wait_recv()

    def tile(cc, k):
        return pl.ds(pl.multiple_of(HALF * cc + 128 * ((x + k) % 4), 128), 128)

    def quant(cols):
        return (base[:, cols].astype(F32) - local[:, cols].astype(F32)).astype(BF16)

    loads[0].wait()
    loads[1].wait()
    order = (2, 1, 3, 0)
    a_id = {k: new_id() for k in order}
    for k in order:
        send_a[k] = quant(tile(1 - c, k))
    pl.semaphore_wait(bar, 24 - 2 * is_self.astype(jnp.int32))
    for k in order:
        send(a_id[k], send_a.at[k], recv_a.at[k], sib)
    for k in order:
        own_q[k] = quant(tile(c, k))

    b_id = {k: new_id() for k in (1, 2, 3)}
    for k in order:
        recv(a_id[k], recv_a.at[k])
        part = own_q[k].astype(F32) + recv_a[k].astype(F32)
        if k:
            send_b[k - 1] = part.astype(BF16)
            send(b_id[k], send_b.at[k - 1], recv_b.at[k - 1], to_x(k))
        else:
            own[...] = part

    loads[2].wait()
    for k in range(4):
        mom_send[k, :, 0:BLK] = mom[:, BLK * k : BLK * (k + 1)]

    def mom_remote(k):
        return pltpu.make_async_remote_copy(
            mom_send.at[k], mom_in.at[qi], mom_ssem.at[k], mom_rsem.at[qi], device_id=mom_dest(k), device_id_type=MESH
        )

    def mom_local(k):
        return pltpu.make_async_copy(mom_send.at[k], mom_in.at[qi], mom_rsem.at[qi])

    for k in range(4):
        mine = jnp.logical_and(is_self, l == k)

        @pl.when(jnp.logical_not(mine))
        def _():
            mom_remote(k).start()

        @pl.when(mine)
        def _():
            mom_local(k).start()

    loads[3].wait()
    loads[4].wait()
    step = 16

    def norm_rows(i, carry):
        at = pl.ds(pl.multiple_of(i * step, step), step)
        v = tok[at, :].astype(F32)
        s = lax.rsqrt(jnp.mean(v * v, axis=1, keepdims=True) + epsilon)
        o = (v * s * gain[...]).astype(BF16)
        for j in range(16):
            nrm[c, j % 4, at, ROWS * (j // 4) : ROWS * (j // 4 + 1)] = o[:, ROWS * j : ROWS * (j + 1)]
        return carry

    lax.fori_loop(0, 7, norm_rows, 0)

    for k in (1, 3, 2):
        recv(b_id[k], recv_b.at[k - 1])
    total = own[...]
    for k in (1, 2, 3):
        total = total + recv_b[k - 1].astype(F32)
    own[...] = total
    send_c[...] = total.astype(BF16)

    def rows80(l_):
        return pl.ds(pl.multiple_of(BLK * l_, 16), BLK)

    c_id = {k: new_id() for k in (1, 2, 3)}
    for k in (1, 2, 3):
        send(c_id[k], send_c.at[rows80((l + k) % 4)], recv_c.at[k - 1], to_l(k))

    for i in range(4):
        pltpu.make_async_copy(mom_send.at[0], mom_in.at[i], mom_rsem.at[i]).wait()
    mom_t[...] = mom_in[...].reshape(128, 128).T
    old = mom_t[0:BLK, :]
    lax.fori_loop(7, 10, norm_rows, 0)

    for k in (1, 3, 2):
        recv(c_id[k], recv_c.at[k - 1])
    pseudo = own[rows80(l), :]
    for k in (1, 2, 3):
        pseudo = pseudo + recv_c[k - 1].astype(F32)
    pseudo = pseudo / REPLICAS
    updated = outer_beta * old + pseudo
    base_own = base[rows80(l), tile(c, 0)].astype(F32)
    w[x, h, y, l] = (base_own - outer_rate * (pseudo + outer_beta * updated)).astype(BF16)

    groups = range(4)
    ring = (2, 1, 3)
    late = (1, 3, 2)
    jump = {k: new_id() for k in ring}
    jump2b = new_id()
    quad = {(g, k): new_id() for g in groups for k in ring}
    ax = {(g, k): new_id() for g in groups for k in ring}
    ay = {(g, k): new_id() for g in groups for k in ring}
    az = {k: new_id(4) for k in ("up", "down", "up2", "down2")}
    one = {(g, d, k): new_id() for g in groups for d in "xy" for k in ring}
    two = {(g, d, k): new_id() for g in groups for d in "xy" for k in ("up", "down", "up2", "down2")}
    a_rows, m_rows = pl.ds(0, A), pl.ds(A, BLK - A)
    lo, hi, every = pl.ds(0, 2), pl.ds(2, 2), pl.ds(0, 4)
    x_step = {"up": 1, "down": 3}

    def grp(g):
        return (h - g) % 4

    def block(g, l_):
        return w.at[x, grp(g), y, l_, m_rows]

    def send_jumps():
        b = w.at[x, h, y, l]
        for k in (1, 3):
            send(jump[k], b, b, to_h(k))

    def wait_jump(g):
        if g == 2:
            recv(jump[2], w.at[x, grp(2), y, l, pl.ds(0, 48)])
            recv(jump2b, w.at[x, grp(2), y, l, pl.ds(48, 32)])
            return
        recv(jump[g], w.at[x, grp(g), y, l])
        part = pl.ds(0, 48) if g == 1 else pl.ds(48, 32)
        b = w.at[x, grp(g), y, l, part]
        send(jump[2] if g == 1 else jump2b, b, b, to_h(g))

    def send_quad(g):
        b = block(g, l)
        for k in ring:
            send(quad[g, k], b, b, to_l(k))

    def wait_quad(g):
        for k in late:
            recv(quad[g, k], block(g, (l - k) % 4))

    def send_ax(g):
        b = w.at[x, grp(g), y, l, a_rows]
        for k in ring:
            send(ax[g, k], b, b, to_x(k))

    def ax_to_ay(g):
        for k in late:
            recv(ax[g, k], w.at[(x - k) % 4, grp(g), y, l, a_rows])
        b = w.at[every, grp(g), y, l, a_rows]
        for k in ring:
            send(ay[g, k], b, b, to_y(k))

    def az_ref(h_, l_, xs=every):
        return w.at[xs, h_, every, l_, a_rows]

    def ay_to_az(g):
        for k in late:
            recv(ay[g, k], w.at[every, grp(g), (y - k) % 4, l, a_rows])
        b = az_ref(grp(g), l)
        send(az["up"] + grp(g), b, b, to_z(1))
        send(az["down"] + grp(g), b, b, to_z(15))
        if g == 2:
            b = az_ref(grp(g), l, lo)
            send(az["up2"] + grp(g), b, b, to_z(2))
            b = az_ref(grp(g), l, hi)
            send(az["down2"] + grp(g), b, b, to_z(14))

    def az_on(g):
        h_ = ((z + 15) % 16 // 4 - g) % 4
        recv(az["up"] + h_, az_ref(h_, (l + 3) % 4))
        b = az_ref(h_, (l + 3) % 4, lo)
        if g != 2:
            send(az["up2"] + h_, b, b, to_z(1))
        h_ = ((z + 1) % 16 // 4 - g) % 4
        recv(az["down"] + h_, az_ref(h_, (l + 1) % 4))
        b = az_ref(h_, (l + 1) % 4, hi)
        if g != 2:
            send(az["down2"] + h_, b, b, to_z(15))

    def az_end(g):
        recv(az["up2"] + grp(g), az_ref(grp(g), (l + 2) % 4, lo))
        recv(az["down2"] + grp(g), az_ref(grp(g), (l + 2) % 4, hi))

    def one_ref(g, d, k):
        if d == "y":
            return w.at[x, grp(g), (y - k) % 4, lo, m_rows]
        return w.at[(x - k) % 4, grp(g), y, hi, m_rows]

    def two_ref(g, d, k, part=every):
        if d == "x":
            return w.at[(x - k) % 4, grp(g), part, lo, m_rows]
        return w.at[part, grp(g), (y - k) % 4, hi, m_rows]

    def send_one(g):
        for k in ring:
            for d, to in (("y", to_y), ("x", to_x)):
                b = one_ref(g, d, 0)
                send(one[g, d, k], b, b, to(k))

    def one_to_two(g):
        for d, e, to in (("y", "x", to_x), ("x", "y", to_y)):
            for k in late:
                recv(one[g, d, k], one_ref(g, d, k))
            b = two_ref(g, e, 0)
            send(two[g, e, "up"], b, b, to(1))
            send(two[g, e, "down"], b, b, to(3))
            if g == 2:
                for key, half in (("up2", lo), ("down2", hi)):
                    b = two_ref(g, e, 0, half)
                    send(two[g, e, key], b, b, to(2))

    def two_on(g):
        for e, to in (("x", to_x), ("y", to_y)):
            recv(two[g, e, "up"], two_ref(g, e, 1))
            b = two_ref(g, e, 1, lo)
            if g != 2:
                send(two[g, e, "up2"], b, b, to(1))
            recv(two[g, e, "down"], two_ref(g, e, 3))
            b = two_ref(g, e, 3, hi)
            if g != 2:
                send(two[g, e, "down2"], b, b, to(3))

    def two_end(g):
        for e in "xy":
            recv(two[g, e, "up2"], two_ref(g, e, 2, lo))
            recv(two[g, e, "down2"], two_ref(g, e, 2, hi))

    def multiply(g, cc, first=False):
        for n in range(2):
            wt = jnp.concatenate([w[2 * n + i, grp(g)].reshape(4 * ROWS, 128) for i in range(2)], axis=1)
            part = jnp.dot(nrm[cc, grp(g)], wt, preferred_element_type=F32)
            cols = slice(256 * n, 256 * (n + 1))
            acc[cc, :, cols] = part if first else acc[cc, :, cols] + part

    send_quad(0)
    send_jumps()
    send_ax(0)

    lax.fori_loop(10, 14, norm_rows, 0)
    ax_to_ay(0)
    wait_quad(0)
    send_one(0)
    for g in (1, 3):
        wait_jump(g)
        send_quad(g)
        send_ax(g)
    lax.fori_loop(14, 16, norm_rows, 0)
    tok_id = new_id()
    send(tok_id, nrm.at[c], nrm.at[c], sib)
    ay_to_az(0)
    one_to_two(0)
    for g in (1, 3):
        ax_to_ay(g)
    for g in (1, 3):
        wait_quad(g)
        send_one(g)
    az_on(0)
    wait_jump(2)
    send_quad(2)
    send_ax(2)
    two_on(0)
    for g in (1, 3):
        ay_to_az(g)
    for g in (1, 3):
        one_to_two(g)
    wait_quad(2)
    send_one(2)
    ax_to_ay(2)
    for g in (1, 3):
        az_on(g)
    ay_to_az(2)
    for g in (1, 3):
        two_on(g)
    one_to_two(2)

    psum[0:BLK, :] = pseudo
    ps_send[...] = psum[...].T

    def ps_remote(i):
        return pltpu.make_async_remote_copy(
            ps_send.at[32 * i : 32 * (i + 1)], ps_recv.at[l], ps_ssem.at[i], ps_rsem.at[l],
            device_id=mom_owner(i), device_id_type=MESH,
        )

    def ps_local(i):
        return pltpu.make_async_copy(ps_send.at[32 * i : 32 * (i + 1)], ps_recv.at[l], ps_rsem.at[l])

    for i in range(4):
        mine = jnp.logical_and(is_self, qi == i)

        @pl.when(jnp.logical_not(mine))
        def _():
            ps_remote(i).start()

        @pl.when(mine)
        def _():
            ps_local(i).start()

    recv(tok_id, nrm.at[1 - c])
    loads[5].wait()
    az_on(2)
    two_on(2)
    two_end(0)
    az_end(0)
    for cc in (0, 1):
        multiply(0, cc, True)
    for g in (1, 3):
        two_end(g)
        az_end(g)
        for cc in (0, 1):
            multiply(g, cc)
    for i in range(4):
        pltpu.make_async_copy(ps_send.at[0:32], ps_recv.at[i], ps_rsem.at[i]).wait()
    for i in range(4):
        nm_ref[:, BLK * i : BLK * (i + 1)] = (
            outer_beta * mom[:, BLK * i : BLK * (i + 1)] + ps_recv[i][:, 0:BLK]
        )

    two_end(2)
    az_end(2)

    my_cols = pl.ds(pl.multiple_of(HALF * c, 128), HALF)
    multiply(2, 1 - c)
    o_send[...] = (acc[1 - c] + bias[:, my_cols]).astype(BF16)
    out_id = new_id()
    send(out_id, o_send, out_ref.at[:, my_cols], sib)
    multiply(2, c)
    out_ref[:, my_cols] = (acc[c] + bias[:, my_cols]).astype(BF16)

    for cp in pending:
        cp.wait_send()
    for k in range(4):
        @pl.when(jnp.logical_not(jnp.logical_and(is_self, l == k)))
        def _():
            mom_remote(k).wait_send()

        @pl.when(jnp.logical_not(jnp.logical_and(is_self, qi == k)))
        def _():
            ps_remote(k).wait_send()
    recv(out_id, out_ref.at[:, pl.ds(pl.multiple_of(HALF * (1 - c), 128), HALF)])
    assert count[0] == TRANSFERS


TRANSFERS = 5 + 3 + 3 + 3 + 12 + 12 + 12 + 16 + 24 + 32 + 2


def per_device(tokens, norm_gain, key_bias, base_weights, local_weights, momentum):
    dma = pltpu.SemaphoreType.DMA
    key_states, new_mom = pl.pallas_call(
        kernel,
        out_shape=(
            pltpu.VMEM((TOK, KV), BF16),
            pltpu.VMEM((32, ROWS), F32),
        ),
        in_specs=[pl.BlockSpec(memory_space=pl.ANY)] * 6,
        out_specs=(pl.BlockSpec(memory_space=pltpu.VMEM), pl.BlockSpec(memory_space=pltpu.VMEM)),
        scratch_shapes=[
            pltpu.VMEM((TOK, D), BF16),
            pltpu.VMEM((1, D), F32),
            pltpu.VMEM((1, KV), F32),
            pltpu.VMEM((ROWS, KV), BF16),
            pltpu.VMEM((ROWS, KV), BF16),
            pltpu.VMEM((32, ROWS), F32),
            pltpu.VMEM((4, 4, 4, 4, BLK, 128), BF16),
            pltpu.VMEM((2, 4, TOK, 4 * ROWS), BF16),
            pltpu.VMEM((2, TOK, HALF), F32),
            pltpu.VMEM((4, ROWS, 128), BF16),
            pltpu.VMEM((4, ROWS, 128), BF16),
            pltpu.VMEM((4, ROWS, 128), BF16),
            pltpu.VMEM((3, ROWS, 128), BF16),
            pltpu.VMEM((3, ROWS, 128), BF16),
            pltpu.VMEM((ROWS, 128), F32),
            pltpu.VMEM((ROWS, 128), BF16),
            pltpu.VMEM((3, BLK, 128), BF16),
            pltpu.VMEM((4, 32, 128), F32),
            pltpu.VMEM((4, 32, 128), F32),
            pltpu.VMEM((128, 128), F32),
            pltpu.VMEM((128, 128), F32),
            pltpu.VMEM((128, 128), F32),
            pltpu.VMEM((4, 32, 128), F32),
            pltpu.VMEM((TOK, HALF), BF16),
            dma((6,)),
            dma((TRANSFERS,)),
            dma((TRANSFERS,)),
            dma((4,)),
            dma((4,)),
            dma((4,)),
            dma((4,)),
        ],
        compiler_params=pltpu.CompilerParams(
            collective_id=0, has_side_effects=True, vmem_limit_bytes=56 * 1024 * 1024
        ),
        name="outer_sync",
    )(
        tokens,
        norm_gain.reshape(1, D),
        key_bias.reshape(1, KV),
        base_weights,
        local_weights.reshape(ROWS, KV),
        momentum.T,
    )
    return (key_states, new_mom.T)


def solution(mesh):
    return jax.shard_map(
        per_device,
        mesh=mesh,
        in_specs=(
            P(("replica", "fsdp"), None),
            P(),
            P(),
            P("fsdp", None),
            P("replica", "fsdp", None),
            P("fsdp", "replica"),
        ),
        out_specs=(P(("replica", "fsdp"), None), P("fsdp", "replica")),
        check_vma=False,
    )
```

```python
import jax
import jax.numpy as jnp
from jax import lax
from jax.experimental import pallas as pl
from jax.experimental.pallas import tpu as pltpu
from jax.sharding import PartitionSpec as P

outer_rate = 0.7
outer_beta = 0.9
epsilon = 1e-06
MESH = pl.DeviceIdType.MESH
F32, BF16 = jnp.float32, jnp.bfloat16
REPLICAS = 32
ROWS, BLK, D, KV, TOK = 320, 80, 5120, 1024, 256
HALF = KV // 2
A = 32


def kernel(
    tok_hbm, gain_hbm, bias_hbm, base_hbm, local_hbm, mom_hbm,
    out_ref, nm_ref,
    tok, gain, bias, base, local, mom,
    w, nrm, acc, send_a, recv_a, own_q, send_b, recv_b, own, send_c, recv_c,
    mom_send, mom_in, mom_t, psum, ps_send, ps_recv, o_send,
    in_sem, ssem, rsem, mom_ssem, mom_rsem, ps_ssem, ps_rsem,
):
    r = lax.axis_index("replica")
    f = lax.axis_index("fsdp")
    x, l, c = r // 8, (r // 2) % 4, r % 2
    y, h = f // 4, f % 4
    z = 4 * h + l
    t = 4 * c + x
    q, qi = r // 4, r % 4
    is_self = q == t

    def rep(x_, l_, c_):
        return (x_ * 4 + l_) * 2 + c_

    def to_x(k):
        return (rep((x + k) % 4, l, c), f)

    def to_y(k):
        return (r, ((y + k) % 4) * 4 + h)

    def to_h(k):
        return (r, y * 4 + (h + k) % 4)

    def to_l(k):
        return (rep(x, (l + k) % 4, c), f)

    def to_z(k):
        z_ = (z + k) % 16
        return (rep(x, z_ % 4, c), y * 4 + z_ // 4)

    sib = (rep(x, l, 1 - c), f)

    loads = []
    for i, (src, dst) in enumerate(
        [(base_hbm, base), (local_hbm, local), (mom_hbm, mom), (tok_hbm, tok), (gain_hbm, gain), (bias_hbm, bias)]
    ):
        cp = pltpu.make_async_copy(src, dst, in_sem.at[i])
        cp.start()
        loads.append(cp)

    bar = pltpu.get_barrier_semaphore()

    def greet(dev):
        pl.semaphore_signal(bar, inc=1, device_id=dev, device_id_type=MESH)

    def mom_dest(k):
        return (rep(q % 4, k, q // 4), f)

    def mom_owner(i):
        return (4 * t + i, f)

    greet(to_h(1))
    greet(to_h(3))
    for k in range(4):
        @pl.when(jnp.logical_not(jnp.logical_and(is_self, l == k)))
        def _():
            greet(mom_dest(k))

        @pl.when(jnp.logical_not(jnp.logical_and(is_self, qi == k)))
        def _():
            greet(mom_owner(k))

    for k in (2, 1, 3):
        greet(to_l(k))
    for k in (2, 1, 3):
        greet(to_x(k))
        greet(to_y(k))
    greet(to_z(1))
    greet(to_z(15))
    greet(to_z(2))
    greet(to_z(14))
    greet(sib)

    count = [0]
    pending = []

    def new_id(n=1):
        count[0] += n
        return count[0] - n

    def remote(i, src, dst, dev):
        return pltpu.make_async_remote_copy(src, dst, ssem.at[i], rsem.at[i], device_id=dev, device_id_type=MESH)

    def send(i, src, dst, dev):
        cp = remote(i, src, dst, dev)
        cp.start()
        pending.append(cp)

    def recv(i, dst):
        remote(i, dst, dst, sib).wait_recv()

    def tile(cc, k):
        return pl.ds(pl.multiple_of(HALF * cc + 128 * ((x + k) % 4), 128), 128)

    def quant(cols):
        return (base[:, cols].astype(F32) - local[:, cols].astype(F32)).astype(BF16)

    loads[0].wait()
    loads[1].wait()
    order = (2, 1, 3, 0)
    a_id = {k: new_id() for k in order}
    for k in order:
        send_a[k] = quant(tile(1 - c, k))
    pl.semaphore_wait(bar, 24 - 2 * is_self.astype(jnp.int32))
    for k in order:
        send(a_id[k], send_a.at[k], recv_a.at[k], sib)
    for k in order:
        own_q[k] = quant(tile(c, k))

    b_id = {k: new_id() for k in (1, 2, 3)}
    for k in order:
        recv(a_id[k], recv_a.at[k])
        part = own_q[k].astype(F32) + recv_a[k].astype(F32)
        if k:
            send_b[k - 1] = part.astype(BF16)
            send(b_id[k], send_b.at[k - 1], recv_b.at[k - 1], to_x(k))
        else:
            own[...] = part

    loads[2].wait()
    for k in range(4):
        mom_send[k, :, 0:BLK] = mom[:, BLK * k : BLK * (k + 1)].astype(BF16)

    def mom_remote(k):
        return pltpu.make_async_remote_copy(
            mom_send.at[k], mom_in.at[qi], mom_ssem.at[k], mom_rsem.at[qi], device_id=mom_dest(k), device_id_type=MESH
        )

    def mom_local(k):
        return pltpu.make_async_copy(mom_send.at[k], mom_in.at[qi], mom_rsem.at[qi])

    for k in range(4):
        mine = jnp.logical_and(is_self, l == k)

        @pl.when(jnp.logical_not(mine))
        def _():
            mom_remote(k).start()

        @pl.when(mine)
        def _():
            mom_local(k).start()

    loads[3].wait()
    loads[4].wait()
    step = 16

    def norm_rows(i, carry):
        at = pl.ds(pl.multiple_of(i * step, step), step)
        v = tok[at, :].astype(F32)
        s = lax.rsqrt(jnp.mean(v * v, axis=1, keepdims=True) + epsilon)
        o = (v * s * gain[...]).astype(BF16)
        for j in range(16):
            nrm[c, j % 4, at, ROWS * (j // 4) : ROWS * (j // 4 + 1)] = o[:, ROWS * j : ROWS * (j + 1)]
        return carry

    lax.fori_loop(0, 7, norm_rows, 0)

    for k in (1, 3, 2):
        recv(b_id[k], recv_b.at[k - 1])
    total = own[...]
    for k in (1, 2, 3):
        total = total + recv_b[k - 1].astype(F32)
    own[...] = total
    send_c[...] = total.astype(BF16)

    def rows80(l_):
        return pl.ds(pl.multiple_of(BLK * l_, 16), BLK)

    c_id = {k: new_id() for k in (1, 2, 3)}
    for k in (1, 2, 3):
        send(c_id[k], send_c.at[rows80((l + k) % 4)], recv_c.at[k - 1], to_l(k))

    for i in range(4):
        pltpu.make_async_copy(mom_send.at[0], mom_in.at[i], mom_rsem.at[i]).wait()
    mom_t[...] = mom_in[...].astype(F32).reshape(128, 128).T
    old = mom_t[0:BLK, :]
    lax.fori_loop(7, 10, norm_rows, 0)

    for k in (1, 3, 2):
        recv(c_id[k], recv_c.at[k - 1])
    pseudo = own[rows80(l), :]
    for k in (1, 2, 3):
        pseudo = pseudo + recv_c[k - 1].astype(F32)
    pseudo = pseudo / REPLICAS
    updated = outer_beta * old + pseudo
    base_own = base[rows80(l), tile(c, 0)].astype(F32)
    w[x, h, y, l] = (base_own - outer_rate * (pseudo + outer_beta * updated)).astype(BF16)

    groups = range(4)
    ring = (2, 1, 3)
    late = (1, 3, 2)
    jump = {k: new_id() for k in ring}
    jump2b = new_id()
    quad = {(g, k): new_id() for g in groups for k in ring}
    ax = {(g, k): new_id() for g in groups for k in ring}
    ay = {(g, k): new_id() for g in groups for k in ring}
    az = {k: new_id(4) for k in ("up", "down", "up2", "down2")}
    one = {(g, d, k): new_id() for g in groups for d in "xy" for k in ring}
    two = {(g, d, k): new_id() for g in groups for d in "xy" for k in ("up", "down", "up2", "down2")}
    a_rows, m_rows = pl.ds(0, A), pl.ds(A, BLK - A)
    lo, hi, every = pl.ds(0, 2), pl.ds(2, 2), pl.ds(0, 4)
    x_step = {"up": 1, "down": 3}

    def grp(g):
        return (h - g) % 4

    def block(g, l_):
        return w.at[x, grp(g), y, l_, m_rows]

    def send_jumps():
        b = w.at[x, h, y, l]
        for k in (1, 3):
            send(jump[k], b, b, to_h(k))

    def wait_jump(g):
        if g == 2:
            recv(jump[2], w.at[x, grp(2), y, l, pl.ds(0, 48)])
            recv(jump2b, w.at[x, grp(2), y, l, pl.ds(48, 32)])
            return
        recv(jump[g], w.at[x, grp(g), y, l])
        part = pl.ds(0, 48) if g == 1 else pl.ds(48, 32)
        b = w.at[x, grp(g), y, l, part]
        send(jump[2] if g == 1 else jump2b, b, b, to_h(g))

    def send_quad(g):
        b = block(g, l)
        for k in ring:
            send(quad[g, k], b, b, to_l(k))

    def wait_quad(g):
        for k in late:
            recv(quad[g, k], block(g, (l - k) % 4))

    def send_ax(g):
        b = w.at[x, grp(g), y, l, a_rows]
        for k in ring:
            send(ax[g, k], b, b, to_x(k))

    def ax_to_ay(g):
        for k in late:
            recv(ax[g, k], w.at[(x - k) % 4, grp(g), y, l, a_rows])
        b = w.at[every, grp(g), y, l, a_rows]
        for k in ring:
            send(ay[g, k], b, b, to_y(k))

    def az_ref(h_, l_, xs=every):
        return w.at[xs, h_, every, l_, a_rows]

    def ay_to_az(g):
        for k in late:
            recv(ay[g, k], w.at[every, grp(g), (y - k) % 4, l, a_rows])
        b = az_ref(grp(g), l)
        send(az["up"] + grp(g), b, b, to_z(1))
        send(az["down"] + grp(g), b, b, to_z(15))
        if g == 2:
            b = az_ref(grp(g), l, lo)
            send(az["up2"] + grp(g), b, b, to_z(2))
            b = az_ref(grp(g), l, hi)
            send(az["down2"] + grp(g), b, b, to_z(14))

    def az_on(g):
        h_ = ((z + 15) % 16 // 4 - g) % 4
        recv(az["up"] + h_, az_ref(h_, (l + 3) % 4))
        b = az_ref(h_, (l + 3) % 4, lo)
        if g != 2:
            send(az["up2"] + h_, b, b, to_z(1))
        h_ = ((z + 1) % 16 // 4 - g) % 4
        recv(az["down"] + h_, az_ref(h_, (l + 1) % 4))
        b = az_ref(h_, (l + 1) % 4, hi)
        if g != 2:
            send(az["down2"] + h_, b, b, to_z(15))

    def az_end(g):
        recv(az["up2"] + grp(g), az_ref(grp(g), (l + 2) % 4, lo))
        recv(az["down2"] + grp(g), az_ref(grp(g), (l + 2) % 4, hi))

    def one_ref(g, d, k):
        if d == "y":
            return w.at[x, grp(g), (y - k) % 4, lo, m_rows]
        return w.at[(x - k) % 4, grp(g), y, hi, m_rows]

    def two_ref(g, d, k, part=every):
        if d == "x":
            return w.at[(x - k) % 4, grp(g), part, lo, m_rows]
        return w.at[part, grp(g), (y - k) % 4, hi, m_rows]

    def send_one(g):
        for k in ring:
            for d, to in (("y", to_y), ("x", to_x)):
                b = one_ref(g, d, 0)
                send(one[g, d, k], b, b, to(k))

    def one_to_two(g):
        for d, e, to in (("y", "x", to_x), ("x", "y", to_y)):
            for k in late:
                recv(one[g, d, k], one_ref(g, d, k))
            b = two_ref(g, e, 0)
            send(two[g, e, "up"], b, b, to(1))
            send(two[g, e, "down"], b, b, to(3))
            if g == 2:
                for key, half in (("up2", lo), ("down2", hi)):
                    b = two_ref(g, e, 0, half)
                    send(two[g, e, key], b, b, to(2))

    def two_on(g):
        for e, to in (("x", to_x), ("y", to_y)):
            recv(two[g, e, "up"], two_ref(g, e, 1))
            b = two_ref(g, e, 1, lo)
            if g != 2:
                send(two[g, e, "up2"], b, b, to(1))
            recv(two[g, e, "down"], two_ref(g, e, 3))
            b = two_ref(g, e, 3, hi)
            if g != 2:
                send(two[g, e, "down2"], b, b, to(3))

    def two_end(g):
        for e in "xy":
            recv(two[g, e, "up2"], two_ref(g, e, 2, lo))
            recv(two[g, e, "down2"], two_ref(g, e, 2, hi))

    def multiply(g, cc, first=False):
        for n in range(2):
            wt = jnp.concatenate([w[2 * n + i, grp(g)].reshape(4 * ROWS, 128) for i in range(2)], axis=1)
            part = jnp.dot(nrm[cc, grp(g)], wt, preferred_element_type=F32)
            cols = slice(256 * n, 256 * (n + 1))
            acc[cc, :, cols] = part if first else acc[cc, :, cols] + part

    send_quad(0)
    send_jumps()
    send_ax(0)

    lax.fori_loop(10, 14, norm_rows, 0)
    ax_to_ay(0)
    wait_quad(0)
    send_one(0)
    for g in (1, 3):
        wait_jump(g)
        send_quad(g)
        send_ax(g)
    lax.fori_loop(14, 16, norm_rows, 0)
    tok_id = new_id()
    send(tok_id, nrm.at[c], nrm.at[c], sib)
    ay_to_az(0)
    one_to_two(0)
    for g in (1, 3):
        ax_to_ay(g)
    for g in (1, 3):
        wait_quad(g)
        send_one(g)
    az_on(0)
    wait_jump(2)
    send_quad(2)
    send_ax(2)
    two_on(0)
    for g in (1, 3):
        ay_to_az(g)
    for g in (1, 3):
        one_to_two(g)
    wait_quad(2)
    send_one(2)
    ax_to_ay(2)
    for g in (1, 3):
        az_on(g)
    ay_to_az(2)
    for g in (1, 3):
        two_on(g)
    one_to_two(2)

    psum[0:BLK, :] = pseudo
    ps_send[...] = psum[...].T.astype(BF16)

    def ps_remote(i):
        return pltpu.make_async_remote_copy(
            ps_send.at[32 * i : 32 * (i + 1)], ps_recv.at[l], ps_ssem.at[i], ps_rsem.at[l],
            device_id=mom_owner(i), device_id_type=MESH,
        )

    def ps_local(i):
        return pltpu.make_async_copy(ps_send.at[32 * i : 32 * (i + 1)], ps_recv.at[l], ps_rsem.at[l])

    for i in range(4):
        mine = jnp.logical_and(is_self, qi == i)

        @pl.when(jnp.logical_not(mine))
        def _():
            ps_remote(i).start()

        @pl.when(mine)
        def _():
            ps_local(i).start()

    recv(tok_id, nrm.at[1 - c])
    loads[5].wait()
    az_on(2)
    two_on(2)
    two_end(0)
    az_end(0)
    for cc in (0, 1):
        multiply(0, cc, True)
    for g in (1, 3):
        two_end(g)
        az_end(g)
        for cc in (0, 1):
            multiply(g, cc)
    for i in range(4):
        pltpu.make_async_copy(ps_send.at[0:32], ps_recv.at[i], ps_rsem.at[i]).wait()
    for i in range(4):
        nm_ref[:, BLK * i : BLK * (i + 1)] = (
            outer_beta * mom[:, BLK * i : BLK * (i + 1)] + ps_recv[i][:, 0:BLK].astype(F32)
        )

    two_end(2)
    az_end(2)

    my_cols = pl.ds(pl.multiple_of(HALF * c, 128), HALF)
    multiply(2, 1 - c)
    o_send[...] = (acc[1 - c] + bias[:, my_cols]).astype(BF16)
    out_id = new_id()
    send(out_id, o_send, out_ref.at[:, my_cols], sib)
    multiply(2, c)
    out_ref[:, my_cols] = (acc[c] + bias[:, my_cols]).astype(BF16)

    for cp in pending:
        cp.wait_send()
    for k in range(4):
        @pl.when(jnp.logical_not(jnp.logical_and(is_self, l == k)))
        def _():
            mom_remote(k).wait_send()

        @pl.when(jnp.logical_not(jnp.logical_and(is_self, qi == k)))
        def _():
            ps_remote(k).wait_send()
    recv(out_id, out_ref.at[:, pl.ds(pl.multiple_of(HALF * (1 - c), 128), HALF)])
    assert count[0] == TRANSFERS


TRANSFERS = 5 + 3 + 3 + 3 + 12 + 12 + 12 + 16 + 24 + 32 + 2


def per_device(tokens, norm_gain, key_bias, base_weights, local_weights, momentum):
    dma = pltpu.SemaphoreType.DMA
    key_states, new_mom = pl.pallas_call(
        kernel,
        out_shape=(
            pltpu.VMEM((TOK, KV), BF16),
            pltpu.VMEM((32, ROWS), F32),
        ),
        in_specs=[pl.BlockSpec(memory_space=pl.ANY)] * 6,
        out_specs=(pl.BlockSpec(memory_space=pltpu.VMEM), pl.BlockSpec(memory_space=pltpu.VMEM)),
        scratch_shapes=[
            pltpu.VMEM((TOK, D), BF16),
            pltpu.VMEM((1, D), F32),
            pltpu.VMEM((1, KV), F32),
            pltpu.VMEM((ROWS, KV), BF16),
            pltpu.VMEM((ROWS, KV), BF16),
            pltpu.VMEM((32, ROWS), F32),
            pltpu.VMEM((4, 4, 4, 4, BLK, 128), BF16),
            pltpu.VMEM((2, 4, TOK, 4 * ROWS), BF16),
            pltpu.VMEM((2, TOK, HALF), F32),
            pltpu.VMEM((4, ROWS, 128), BF16),
            pltpu.VMEM((4, ROWS, 128), BF16),
            pltpu.VMEM((4, ROWS, 128), BF16),
            pltpu.VMEM((3, ROWS, 128), BF16),
            pltpu.VMEM((3, ROWS, 128), BF16),
            pltpu.VMEM((ROWS, 128), F32),
            pltpu.VMEM((ROWS, 128), BF16),
            pltpu.VMEM((3, BLK, 128), BF16),
            pltpu.VMEM((4, 32, 128), BF16),
            pltpu.VMEM((4, 32, 128), BF16),
            pltpu.VMEM((128, 128), F32),
            pltpu.VMEM((128, 128), F32),
            pltpu.VMEM((128, 128), BF16),
            pltpu.VMEM((4, 32, 128), BF16),
            pltpu.VMEM((TOK, HALF), BF16),
            dma((6,)),
            dma((TRANSFERS,)),
            dma((TRANSFERS,)),
            dma((4,)),
            dma((4,)),
            dma((4,)),
            dma((4,)),
        ],
        compiler_params=pltpu.CompilerParams(
            collective_id=0, has_side_effects=True, vmem_limit_bytes=56 * 1024 * 1024
        ),
        name="outer_sync",
    )(
        tokens,
        norm_gain.reshape(1, D),
        key_bias.reshape(1, KV),
        base_weights,
        local_weights.reshape(ROWS, KV),
        momentum.T,
    )
    return (key_states, new_mom.T)


def solution(mesh):
    return jax.shard_map(
        per_device,
        mesh=mesh,
        in_specs=(
            P(("replica", "fsdp"), None),
            P(),
            P(),
            P("fsdp", None),
            P("replica", "fsdp", None),
            P("fsdp", "replica"),
        ),
        out_specs=(P(("replica", "fsdp"), None), P("fsdp", "replica")),
        check_vma=False,
    )
```

```python
import jax
import jax.numpy as jnp
from jax import lax
from jax.experimental import pallas as pl
from jax.experimental.pallas import tpu as pltpu
from jax.sharding import PartitionSpec as P

outer_rate = 0.7
outer_beta = 0.9
epsilon = 1e-06
MESH = pl.DeviceIdType.MESH
F32, BF16 = jnp.float32, jnp.bfloat16
REPLICAS = 32
ROWS, BLK, D, KV, TOK = 320, 80, 5120, 1024, 256
HALF = KV // 2
A = 32


def kernel(
    tok_hbm, gain_hbm, bias_hbm, base_hbm, local_hbm, mom_hbm,
    out_ref, nm_ref,
    tok, gain, bias, base, local, mom,
    w, nrm, acc, send_a, recv_a, own_q, send_b, recv_b, own, send_c, recv_c,
    mom_send, mom_in, mom_t, psum, ps_send, ps_recv, o_send,
    in_sem, ssem, rsem, mom_ssem, mom_rsem, ps_ssem, ps_rsem,
):
    r = lax.axis_index("replica")
    f = lax.axis_index("fsdp")
    x, l, c = r // 8, (r // 2) % 4, r % 2
    y, h = f // 4, f % 4
    z = 4 * h + l
    t = 4 * c + x
    q, qi = r // 4, r % 4
    is_self = q == t

    def rep(x_, l_, c_):
        return (x_ * 4 + l_) * 2 + c_

    def to_x(k):
        return (rep((x + k) % 4, l, c), f)

    def to_y(k):
        return (r, ((y + k) % 4) * 4 + h)

    def to_h(k):
        return (r, y * 4 + (h + k) % 4)

    def to_l(k):
        return (rep(x, (l + k) % 4, c), f)

    def to_z(k):
        z_ = (z + k) % 16
        return (rep(x, z_ % 4, c), y * 4 + z_ // 4)

    sib = (rep(x, l, 1 - c), f)

    loads = []
    for i, (src, dst) in enumerate(
        [(base_hbm, base), (local_hbm, local), (mom_hbm, mom), (tok_hbm, tok), (gain_hbm, gain), (bias_hbm, bias)]
    ):
        cp = pltpu.make_async_copy(src, dst, in_sem.at[i])
        cp.start()
        loads.append(cp)

    bar = pltpu.get_barrier_semaphore()

    def greet(dev):
        pl.semaphore_signal(bar, inc=1, device_id=dev, device_id_type=MESH)

    def mom_dest(k):
        return (rep(q % 4, k, q // 4), f)

    def mom_owner(i):
        return (4 * t + i, f)

    greet(to_h(1))
    greet(to_h(3))
    for k in range(4):
        @pl.when(jnp.logical_not(jnp.logical_and(is_self, l == k)))
        def _():
            greet(mom_dest(k))

        @pl.when(jnp.logical_not(jnp.logical_and(is_self, qi == k)))
        def _():
            greet(mom_owner(k))

    for k in (2, 1, 3):
        greet(to_l(k))
    for k in (2, 1, 3):
        greet(to_x(k))
        greet(to_y(k))
    greet(to_z(1))
    greet(to_z(15))
    greet(to_z(2))
    greet(to_z(14))
    greet(sib)

    count = [0]
    pending = []

    def new_id(n=1):
        count[0] += n
        return count[0] - n

    def remote(i, src, dst, dev):
        return pltpu.make_async_remote_copy(src, dst, ssem.at[i], rsem.at[i], device_id=dev, device_id_type=MESH)

    def send(i, src, dst, dev):
        cp = remote(i, src, dst, dev)
        cp.start()
        pending.append(cp)

    def recv(i, dst):
        remote(i, dst, dst, sib).wait_recv()

    def tile(cc, k):
        return pl.ds(pl.multiple_of(HALF * cc + 128 * ((x + k) % 4), 128), 128)

    def quant(cols):
        return (base[:, cols].astype(F32) - local[:, cols].astype(F32)).astype(BF16)

    loads[0].wait()
    loads[1].wait()
    order = (2, 1, 3, 0)
    a_id = {k: new_id() for k in order}
    for k in order:
        send_a[k] = quant(tile(1 - c, k))
    pl.semaphore_wait(bar, 24 - 2 * is_self.astype(jnp.int32))
    for k in order:
        send(a_id[k], send_a.at[k], recv_a.at[k], sib)
    for k in order:
        own_q[k] = quant(tile(c, k))

    b_id = {k: new_id() for k in (1, 2, 3)}
    for k in order:
        recv(a_id[k], recv_a.at[k])
        part = own_q[k].astype(F32) + recv_a[k].astype(F32)
        if k:
            send_b[k - 1] = part.astype(BF16)
            send(b_id[k], send_b.at[k - 1], recv_b.at[k - 1], to_x(k))
        else:
            own[...] = part

    loads[3].wait()
    loads[4].wait()
    step = 16

    def norm_rows(i, carry):
        at = pl.ds(pl.multiple_of(i * step, step), step)
        v = tok[at, :].astype(F32)
        s = lax.rsqrt(jnp.mean(v * v, axis=1, keepdims=True) + epsilon)
        o = (v * s * gain[...]).astype(BF16)
        for j in range(16):
            nrm[c, j % 4, at, ROWS * (j // 4) : ROWS * (j // 4 + 1)] = o[:, ROWS * j : ROWS * (j + 1)]
        return carry

    lax.fori_loop(0, 7, norm_rows, 0)

    loads[2].wait()
    for k in range(4):
        mom_send[k, :, 0:BLK] = mom[:, BLK * k : BLK * (k + 1)].astype(BF16)

    def mom_remote(k):
        return pltpu.make_async_remote_copy(
            mom_send.at[k], mom_in.at[qi], mom_ssem.at[k], mom_rsem.at[qi], device_id=mom_dest(k), device_id_type=MESH
        )

    def mom_local(k):
        return pltpu.make_async_copy(mom_send.at[k], mom_in.at[qi], mom_rsem.at[qi])

    for k in range(4):
        mine = jnp.logical_and(is_self, l == k)

        @pl.when(jnp.logical_not(mine))
        def _():
            mom_remote(k).start()

        @pl.when(mine)
        def _():
            mom_local(k).start()

    for k in (1, 3, 2):
        recv(b_id[k], recv_b.at[k - 1])
    total = own[...]
    for k in (1, 2, 3):
        total = total + recv_b[k - 1].astype(F32)
    own[...] = total
    send_c[...] = total.astype(BF16)

    def rows80(l_):
        return pl.ds(pl.multiple_of(BLK * l_, 16), BLK)

    c_id = {k: new_id() for k in (1, 2, 3)}
    for k in (1, 2, 3):
        send(c_id[k], send_c.at[rows80((l + k) % 4)], recv_c.at[k - 1], to_l(k))

    for i in range(4):
        pltpu.make_async_copy(mom_send.at[0], mom_in.at[i], mom_rsem.at[i]).wait()
    mom_t[...] = mom_in[...].astype(F32).reshape(128, 128).T
    old = mom_t[0:BLK, :]
    lax.fori_loop(7, 10, norm_rows, 0)

    for k in (1, 3, 2):
        recv(c_id[k], recv_c.at[k - 1])
    pseudo = own[rows80(l), :]
    for k in (1, 2, 3):
        pseudo = pseudo + recv_c[k - 1].astype(F32)
    pseudo = pseudo / REPLICAS
    updated = outer_beta * old + pseudo
    base_own = base[rows80(l), tile(c, 0)].astype(F32)
    w[x, h, y, l] = (base_own - outer_rate * (pseudo + outer_beta * updated)).astype(BF16)

    groups = range(4)
    ring = (2, 1, 3)
    late = (1, 3, 2)
    jump = {k: new_id() for k in ring}
    jump2b = new_id()
    quad = {(g, k): new_id() for g in groups for k in ring}
    ax = {(g, k): new_id() for g in groups for k in ring}
    ay = {(g, k): new_id() for g in groups for k in ring}
    az = {k: new_id(4) for k in ("up", "down", "up2", "down2")}
    one = {(g, d, k): new_id() for g in groups for d in "xy" for k in ring}
    two = {(g, d, k): new_id() for g in groups for d in "xy" for k in ("up", "down", "up2", "down2")}
    a_rows, m_rows = pl.ds(0, A), pl.ds(A, BLK - A)
    lo, hi, every = pl.ds(0, 2), pl.ds(2, 2), pl.ds(0, 4)
    x_step = {"up": 1, "down": 3}

    def grp(g):
        return (h - g) % 4

    def block(g, l_):
        return w.at[x, grp(g), y, l_, m_rows]

    def send_jumps():
        b = w.at[x, h, y, l]
        for k in (1, 3):
            send(jump[k], b, b, to_h(k))

    def wait_jump(g):
        if g == 2:
            recv(jump[2], w.at[x, grp(2), y, l, pl.ds(0, 48)])
            recv(jump2b, w.at[x, grp(2), y, l, pl.ds(48, 32)])
            return
        recv(jump[g], w.at[x, grp(g), y, l])
        part = pl.ds(0, 48) if g == 1 else pl.ds(48, 32)
        b = w.at[x, grp(g), y, l, part]
        send(jump[2] if g == 1 else jump2b, b, b, to_h(g))

    def send_quad(g):
        b = block(g, l)
        for k in ring:
            send(quad[g, k], b, b, to_l(k))

    def wait_quad(g):
        for k in late:
            recv(quad[g, k], block(g, (l - k) % 4))

    def send_ax(g):
        b = w.at[x, grp(g), y, l, a_rows]
        for k in ring:
            send(ax[g, k], b, b, to_x(k))

    def ax_to_ay(g):
        for k in late:
            recv(ax[g, k], w.at[(x - k) % 4, grp(g), y, l, a_rows])
        b = w.at[every, grp(g), y, l, a_rows]
        for k in ring:
            send(ay[g, k], b, b, to_y(k))

    def az_ref(h_, l_, xs=every):
        return w.at[xs, h_, every, l_, a_rows]

    def ay_to_az(g):
        for k in late:
            recv(ay[g, k], w.at[every, grp(g), (y - k) % 4, l, a_rows])
        b = az_ref(grp(g), l)
        send(az["up"] + grp(g), b, b, to_z(1))
        send(az["down"] + grp(g), b, b, to_z(15))
        if g == 2:
            b = az_ref(grp(g), l, lo)
            send(az["up2"] + grp(g), b, b, to_z(2))
            b = az_ref(grp(g), l, hi)
            send(az["down2"] + grp(g), b, b, to_z(14))

    def az_on(g):
        h_ = ((z + 15) % 16 // 4 - g) % 4
        recv(az["up"] + h_, az_ref(h_, (l + 3) % 4))
        b = az_ref(h_, (l + 3) % 4, lo)
        if g != 2:
            send(az["up2"] + h_, b, b, to_z(1))
        h_ = ((z + 1) % 16 // 4 - g) % 4
        recv(az["down"] + h_, az_ref(h_, (l + 1) % 4))
        b = az_ref(h_, (l + 1) % 4, hi)
        if g != 2:
            send(az["down2"] + h_, b, b, to_z(15))

    def az_end(g):
        recv(az["up2"] + grp(g), az_ref(grp(g), (l + 2) % 4, lo))
        recv(az["down2"] + grp(g), az_ref(grp(g), (l + 2) % 4, hi))

    def one_ref(g, d, k):
        if d == "y":
            return w.at[x, grp(g), (y - k) % 4, lo, m_rows]
        return w.at[(x - k) % 4, grp(g), y, hi, m_rows]

    def two_ref(g, d, k, part=every):
        if d == "x":
            return w.at[(x - k) % 4, grp(g), part, lo, m_rows]
        return w.at[part, grp(g), (y - k) % 4, hi, m_rows]

    def send_one(g):
        for k in ring:
            for d, to in (("y", to_y), ("x", to_x)):
                b = one_ref(g, d, 0)
                send(one[g, d, k], b, b, to(k))

    def one_to_two(g):
        for d, e, to in (("y", "x", to_x), ("x", "y", to_y)):
            for k in late:
                recv(one[g, d, k], one_ref(g, d, k))
            b = two_ref(g, e, 0)
            send(two[g, e, "up"], b, b, to(1))
            send(two[g, e, "down"], b, b, to(3))
            if g == 2:
                for key, half in (("up2", lo), ("down2", hi)):
                    b = two_ref(g, e, 0, half)
                    send(two[g, e, key], b, b, to(2))

    def two_on(g):
        for e, to in (("x", to_x), ("y", to_y)):
            recv(two[g, e, "up"], two_ref(g, e, 1))
            b = two_ref(g, e, 1, lo)
            if g != 2:
                send(two[g, e, "up2"], b, b, to(1))
            recv(two[g, e, "down"], two_ref(g, e, 3))
            b = two_ref(g, e, 3, hi)
            if g != 2:
                send(two[g, e, "down2"], b, b, to(3))

    def two_end(g):
        for e in "xy":
            recv(two[g, e, "up2"], two_ref(g, e, 2, lo))
            recv(two[g, e, "down2"], two_ref(g, e, 2, hi))

    def multiply(g, cc, first=False):
        for n in range(2):
            wt = jnp.concatenate([w[2 * n + i, grp(g)].reshape(4 * ROWS, 128) for i in range(2)], axis=1)
            part = jnp.dot(nrm[cc, grp(g)], wt, preferred_element_type=F32)
            cols = slice(256 * n, 256 * (n + 1))
            acc[cc, :, cols] = part if first else acc[cc, :, cols] + part

    send_quad(0)
    send_jumps()
    send_ax(0)

    lax.fori_loop(10, 14, norm_rows, 0)
    ax_to_ay(0)
    wait_quad(0)
    send_one(0)
    for g in (1, 3):
        wait_jump(g)
        send_quad(g)
        send_ax(g)
    lax.fori_loop(14, 16, norm_rows, 0)
    tok_id = new_id()
    send(tok_id, nrm.at[c], nrm.at[c], sib)
    ay_to_az(0)
    one_to_two(0)
    for g in (1, 3):
        ax_to_ay(g)
    for g in (1, 3):
        wait_quad(g)
        send_one(g)
    az_on(0)
    wait_jump(2)
    send_quad(2)
    send_ax(2)
    two_on(0)
    for g in (1, 3):
        ay_to_az(g)
    for g in (1, 3):
        one_to_two(g)
    wait_quad(2)
    send_one(2)
    ax_to_ay(2)
    for g in (1, 3):
        az_on(g)
    ay_to_az(2)
    for g in (1, 3):
        two_on(g)
    one_to_two(2)

    psum[0:BLK, :] = pseudo
    ps_send[...] = psum[...].T.astype(BF16)

    def ps_remote(i):
        return pltpu.make_async_remote_copy(
            ps_send.at[32 * i : 32 * (i + 1)], ps_recv.at[l], ps_ssem.at[i], ps_rsem.at[l],
            device_id=mom_owner(i), device_id_type=MESH,
        )

    def ps_local(i):
        return pltpu.make_async_copy(ps_send.at[32 * i : 32 * (i + 1)], ps_recv.at[l], ps_rsem.at[l])

    for i in range(4):
        mine = jnp.logical_and(is_self, qi == i)

        @pl.when(jnp.logical_not(mine))
        def _():
            ps_remote(i).start()

        @pl.when(mine)
        def _():
            ps_local(i).start()

    recv(tok_id, nrm.at[1 - c])
    loads[5].wait()
    az_on(2)
    two_on(2)
    two_end(0)
    az_end(0)
    for cc in (0, 1):
        multiply(0, cc, True)
    for g in (1, 3):
        two_end(g)
        az_end(g)
        for cc in (0, 1):
            multiply(g, cc)
    for i in range(4):
        pltpu.make_async_copy(ps_send.at[0:32], ps_recv.at[i], ps_rsem.at[i]).wait()
    for i in range(4):
        nm_ref[:, BLK * i : BLK * (i + 1)] = (
            outer_beta * mom[:, BLK * i : BLK * (i + 1)] + ps_recv[i][:, 0:BLK].astype(F32)
        )

    two_end(2)
    az_end(2)

    my_cols = pl.ds(pl.multiple_of(HALF * c, 128), HALF)
    multiply(2, 1 - c)
    o_send[...] = (acc[1 - c] + bias[:, my_cols]).astype(BF16)
    out_id = new_id()
    send(out_id, o_send, out_ref.at[:, my_cols], sib)
    multiply(2, c)
    out_ref[:, my_cols] = (acc[c] + bias[:, my_cols]).astype(BF16)

    for cp in pending:
        cp.wait_send()
    for k in range(4):
        @pl.when(jnp.logical_not(jnp.logical_and(is_self, l == k)))
        def _():
            mom_remote(k).wait_send()

        @pl.when(jnp.logical_not(jnp.logical_and(is_self, qi == k)))
        def _():
            ps_remote(k).wait_send()
    recv(out_id, out_ref.at[:, pl.ds(pl.multiple_of(HALF * (1 - c), 128), HALF)])
    assert count[0] == TRANSFERS


TRANSFERS = 5 + 3 + 3 + 3 + 12 + 12 + 12 + 16 + 24 + 32 + 2


def per_device(tokens, norm_gain, key_bias, base_weights, local_weights, momentum):
    dma = pltpu.SemaphoreType.DMA
    key_states, new_mom = pl.pallas_call(
        kernel,
        out_shape=(
            pltpu.VMEM((TOK, KV), BF16),
            pltpu.VMEM((32, ROWS), F32),
        ),
        in_specs=[pl.BlockSpec(memory_space=pl.ANY)] * 6,
        out_specs=(pl.BlockSpec(memory_space=pltpu.VMEM), pl.BlockSpec(memory_space=pltpu.VMEM)),
        scratch_shapes=[
            pltpu.VMEM((TOK, D), BF16),
            pltpu.VMEM((1, D), F32),
            pltpu.VMEM((1, KV), F32),
            pltpu.VMEM((ROWS, KV), BF16),
            pltpu.VMEM((ROWS, KV), BF16),
            pltpu.VMEM((32, ROWS), F32),
            pltpu.VMEM((4, 4, 4, 4, BLK, 128), BF16),
            pltpu.VMEM((2, 4, TOK, 4 * ROWS), BF16),
            pltpu.VMEM((2, TOK, HALF), F32),
            pltpu.VMEM((4, ROWS, 128), BF16),
            pltpu.VMEM((4, ROWS, 128), BF16),
            pltpu.VMEM((4, ROWS, 128), BF16),
            pltpu.VMEM((3, ROWS, 128), BF16),
            pltpu.VMEM((3, ROWS, 128), BF16),
            pltpu.VMEM((ROWS, 128), F32),
            pltpu.VMEM((ROWS, 128), BF16),
            pltpu.VMEM((3, BLK, 128), BF16),
            pltpu.VMEM((4, 32, 128), BF16),
            pltpu.VMEM((4, 32, 128), BF16),
            pltpu.VMEM((128, 128), F32),
            pltpu.VMEM((128, 128), F32),
            pltpu.VMEM((128, 128), BF16),
            pltpu.VMEM((4, 32, 128), BF16),
            pltpu.VMEM((TOK, HALF), BF16),
            dma((6,)),
            dma((TRANSFERS,)),
            dma((TRANSFERS,)),
            dma((4,)),
            dma((4,)),
            dma((4,)),
            dma((4,)),
        ],
        compiler_params=pltpu.CompilerParams(
            collective_id=0, has_side_effects=True, vmem_limit_bytes=56 * 1024 * 1024
        ),
        name="outer_sync",
    )(
        tokens,
        norm_gain.reshape(1, D),
        key_bias.reshape(1, KV),
        base_weights,
        local_weights.reshape(ROWS, KV),
        momentum.T,
    )
    return (key_states, new_mom.T)


def solution(mesh):
    return jax.shard_map(
        per_device,
        mesh=mesh,
        in_specs=(
            P(("replica", "fsdp"), None),
            P(),
            P(),
            P("fsdp", None),
            P("replica", "fsdp", None),
            P("fsdp", "replica"),
        ),
        out_specs=(P(("replica", "fsdp"), None), P("fsdp", "replica")),
        check_vma=False,
    )
```
